128 devices in a mesh: ctx: 16 (over z, y_lo, core), head: 8 (over x, y_hi).
Axes of the slice: x: 4, y: 4 (y_hi: 2, y_lo: 2; y = y_hi * 2 + y_lo), z: 4, core: 2. Of those that a mesh axis runs over, the one named last changes fastest.
Arguments:
- x_in: bfloat16 [2, 6144, 8192], P(None, 'ctx', 'head'), as said below
- z_in: bfloat16 [2, 6144, 8192], P(None, 'ctx', 'head'), may hold values from -6 to 6
- bc_in: bfloat16 [2, 6144, 2, 1024], P(None, 'ctx', None, 'head'), may hold values from -6 to 6
- conv_x: float32 [4, 8192], P(None, 'head'), may hold values from -3 to 3
- conv_bc: float32 [4, 2, 1024], P(None, None, 'head'), may hold values from -3 to 3
- dt_raw: float32 [2, 128, 6144], P(None, 'head', 'ctx'), as said below
- a_log: float32 [128], P('head'), as said below
- skip_scale: float32 [128], P('head'), may hold values from 0.3 to 3
- norm_gain: float32 [8192], P('head'), may hold values from 0.25 to 1.75
- out_weight: bfloat16 [8192, 8192], P('head'), may hold values from -0.09375 to 0.09375
Outputs:
- layer_out: bfloat16 [2, 6144, 8192], P(None, 'ctx', 'head')
The draws below stay inside these ranges and needn't reach their ends.
Inputs may be any that keep to these rules, and one draw needn't show every extreme that they name: `x_in`: one value a position and channel. `dt_raw`: one value a sequence, head and position. `a_log`: one value a head.
All inputs are finite; a program needn't handle non-finite values.
Results may differ from the reference program's by a relative error of at most 0.034.
Values may be sent and summed in bfloat16 or wider, within the bound.
A program may use at most 128 MiB of HBM per device.

```python
import math
import jax
import jax.numpy as jnp
from jax import lax

D = 8192
HEADS = 128
HEAD_DIM = 64
STATE = 128
GROUPS = 8
KW = 4
BATCH_COUNT = 2
INNER = 8192
HALF = 192
CONTEXT_SPAN = 6144
N_CTX = 16
N_HEAD = 8


def head_plan(key, slow_share):
    key_kind, key_slow, key_fast = jax.random.split(key, 3)
    delayed_channels = jax.random.uniform(key_kind, (HEADS,)) < slow_share
    slow_rate = jnp.exp(jax.random.uniform(key_slow, (HEADS,), minval=math.log(0.2), maxval=0.0)) / (CONTEXT_SPAN * 0.07)
    fast_rate = jnp.exp(jax.random.uniform(key_fast, (HEADS,), minval=math.log(0.3), maxval=math.log(0.8)))
    return (delayed_channels, jnp.where(delayed_channels, slow_rate, fast_rate))


def draw_a_log(key, part):
    slow_share = 0.5
    delayed_channels, rate_coeff = head_plan(key, slow_share)
    return jnp.log(rate_coeff).astype(jnp.float32)


def draw_dt_raw(key, part):
    slow_share = 0.5
    delayed_channels, rate_coeff = head_plan(key, slow_share)
    key = jax.random.fold_in(key, 12)
    key_jitter, key_offset, random_seed_place, key_lost = jax.random.split(key, 4)
    shape_all = (BATCH_COUNT, HEADS, CONTEXT_SPAN)
    jitter = jnp.clip(0.5 * jax.random.normal(key_jitter, shape_all), -1.5, 1.5)
    offset = jax.random.uniform(key_offset, (HEADS,), minval=-0.6, maxval=0.6)
    steady_amount = -2.6 + offset[None, :, None] + jitter
    spike_place = jax.random.randint(random_seed_place, (BATCH_COUNT, 3, 1), 0, CONTEXT_SPAN)
    paired_lines = jnp.any(spike_place == jnp.arange(CONTEXT_SPAN)[None, None, :], axis=1)
    lost_share = jax.random.uniform(key_lost, shape_all, minval=0.2, maxval=0.5)
    target_number = -jnp.log1p(-lost_share) / rate_coeff[None, :, None]
    spike_drawn = target_number + jnp.log(-jnp.expm1(-target_number))
    selected_channels = jnp.where(delayed_channels[None, :, None] & paired_lines[:, None, :], spike_drawn, steady_amount)
    return selected_channels.astype(jnp.float32)


def draw_x_in(key, part):
    key = jax.random.fold_in(key, 13)
    key_base, key_rows, key_cols = jax.random.split(key, 3)
    shape_all = (BATCH_COUNT, CONTEXT_SPAN, HEADS * HEAD_DIM)
    row_scale = jnp.exp(jax.random.uniform(key_rows, (BATCH_COUNT, CONTEXT_SPAN, 1), minval=math.log(0.35), maxval=math.log(2.8)))
    col_scale = jnp.exp(jax.random.uniform(key_cols, (1, 1, HEADS * HEAD_DIM), minval=math.log(0.35), maxval=math.log(2.8)))
    drawn_base = jnp.clip(jax.random.normal(key_base, shape_all), -4.0, 4.0)
    return (drawn_base * row_scale * col_scale).astype(jnp.bfloat16)


def raised(values, stream_key, source, target, parts, factor):
    def block_of(axis_at):
        return (jnp.arange(values.shape[axis_at]) // (values.shape[axis_at] // parts)).reshape((-1,) + (1,) * (values.ndim - 1 - axis_at))

    one_side = jax.random.permutation(stream_key, parts)[block_of(target)]
    second = (block_of(target) + parts // 2) % parts
    return jnp.where((block_of(source) == one_side) | (block_of(source) == second), factor * values, values)


def block_scale(rng, shape, pieces, least, largest):
    def one(dim, parts):
        steps = jax.random.uniform(jax.random.fold_in(jax.random.fold_in(rng, 6), dim), (parts,), jnp.float32, least / len(pieces), largest / len(pieces))
        return jnp.repeat(jnp.exp(steps), shape[dim] // parts).reshape((-1,) + (1,) * (len(shape) - dim - 1))

    factor_of = one(*pieces[0])
    for cut in pieces[1:]:
        factor_of = factor_of * one(*cut)
    return factor_of


def scatter_about(own_key, dims, deviation, reach, cuts=(), held_as=jnp.bfloat16):
    values = jax.random.normal(own_key, dims, jnp.float32) * deviation
    if len(cuts) > 0:
        values = block_scale(own_key, dims, cuts, -0.22, 0.18) * values
    return jnp.clip(values, min=-reach, max=reach).astype(held_as)


def heavy_noise(own_key, dims, scale, limit, shards, heavy, held_as=jnp.bfloat16):
    array = scale * jax.random.normal(own_key, dims, jnp.float32)
    if shards:
        array = array * block_scale(own_key, dims, shards, -0.22, 0.18)
    return jnp.clip(raised(array, jax.random.fold_in(own_key, 3), *heavy), -limit, limit).astype(held_as)


def setup_inputs(seed: int = 0) -> dict:
    streams_of = jax.random.split(jax.random.key(seed), 11)
    x_in = draw_x_in(jax.random.fold_in(streams_of[10], 71), 0)
    z_in = scatter_about(streams_of[1], (BATCH_COUNT, CONTEXT_SPAN, INNER), 1.0, 6.0, ((1, 16), (2, 8)))
    bc_in = scatter_about(streams_of[2], (BATCH_COUNT, CONTEXT_SPAN, 2, GROUPS * STATE), 1.0, 6.0, ((1, 16), (3, 8)))
    conv_x = scatter_about(streams_of[3], (KW, INNER), KW ** -0.5, 3.0, ((1, 8),), jnp.float32)
    conv_bc = scatter_about(streams_of[4], (KW, 2, GROUPS * STATE), KW ** -0.5, 3.0, ((2, 8),), jnp.float32)
    dt_raw = draw_dt_raw(jax.random.fold_in(streams_of[10], 71), 0)
    a_log = draw_a_log(jax.random.fold_in(streams_of[10], 71), 0)
    skip_scale = jnp.clip(jnp.exp(math.log(3.0) - 2.3025851 * jax.random.uniform(streams_of[7], (HEADS,), jnp.float32) ** block_scale(streams_of[7], (HEADS,), ((0, 8),), -0.2, 0.2)), 0.3, 3.0)
    norm_gain = jnp.clip(1.0 + 0.15 * jax.random.normal(streams_of[8], (INNER,), jnp.float32), 0.25, 1.75)
    out_weight = heavy_noise(streams_of[9], (INNER, D), INNER ** -0.5, 0.09375, ((0, 8),), (0, 1, 8, 2.0))
    return dict(x_in=x_in, z_in=z_in, bc_in=bc_in, conv_x=conv_x, conv_bc=conv_bc, dt_raw=dt_raw, a_log=a_log, skip_scale=skip_scale, norm_gain=norm_gain, out_weight=out_weight)


def to_blocks(stored):
    shaped = stored.reshape((stored.shape[0], N_CTX, 2, HALF) + stored.shape[2:])
    return jnp.concatenate([shaped[:, :, 0], jnp.flip(shaped[:, :, 1], axis=1)], axis=1)

def from_blocks(ordered):
    lower_half = ordered[:, :N_CTX]
    upper_half = jnp.flip(ordered[:, N_CTX:], axis=1)
    paired = jnp.stack([lower_half, upper_half], axis=2)
    return paired.reshape((ordered.shape[0], N_CTX * 2 * HALF) + ordered.shape[3:])

def sigmoid_gate(values):
    return values / (1.0 + jnp.exp(-values))

def widened(values):
    return lax.optimization_barrier(values).astype(jnp.float32)

def reference(x_in, z_in, bc_in, conv_x, conv_bc, dt_raw, a_log, skip_scale, norm_gain, out_weight):
    per_group = HEADS // GROUPS
    group_cols = GROUPS * STATE
    block_count = 2 * N_CTX
    joined = jnp.concatenate([x_in, bc_in.reshape(BATCH_COUNT, CONTEXT_SPAN, 2 * group_cols)], axis=2)
    ordered = to_blocks(joined).reshape(BATCH_COUNT, CONTEXT_SPAN, INNER + 2 * group_cols)
    padded = jnp.pad(ordered, ((0, 0), (KW - 1, 0), (0, 0)))
    conv_taps = jnp.concatenate([conv_x, conv_bc.reshape(KW, 2 * group_cols)], axis=1)
    summed = jnp.zeros((BATCH_COUNT, CONTEXT_SPAN, INNER + 2 * group_cols), jnp.float32)
    for tap_index in range(KW):
        summed = summed + conv_taps[tap_index] * padded[:, tap_index:tap_index + CONTEXT_SPAN].astype(jnp.float32)
    conv_out = sigmoid_gate(summed).astype(jnp.bfloat16)
    xs_all = conv_out[:, :, :INNER].reshape(BATCH_COUNT, block_count, HALF, HEADS, HEAD_DIM)
    bs_all = conv_out[:, :, INNER:INNER + group_cols].reshape(BATCH_COUNT, block_count, HALF, GROUPS, STATE)
    cs_all = conv_out[:, :, INNER + group_cols:].reshape(BATCH_COUNT, block_count, HALF, GROUPS, STATE)
    step_size = to_blocks(jax.nn.softplus(dt_raw).transpose(0, 2, 1))
    log_fall = step_size * -jnp.exp(a_log)
    cumulative = jnp.cumsum(log_fall, axis=2)
    causal = jnp.tril(jnp.ones((HALF, HALF), dtype=bool))

    def advance(entry_state, block_data):
        xs_k, bs_k, cs_k, step_k, cum_k = block_data
        scores = jnp.einsum('sqgn,sugn->sgqu', cs_k.astype(jnp.float32), bs_k.astype(jnp.float32))
        scores = jnp.repeat(scores, per_group, axis=1)
        cum_t = cum_k.transpose(0, 2, 1)
        step_t = step_k.transpose(0, 2, 1)
        gap_matrix = cum_t[:, :, :, None] - cum_t[:, :, None, :]
        factor = jnp.where(causal, jnp.exp(jnp.where(causal, gap_matrix, 0.0)), 0.0)
        weights = (scores * factor * step_t[:, :, None, :]).astype(jnp.bfloat16)
        intra_part = jnp.einsum('shqu,suhp->sqhp', widened(weights), xs_k.astype(jnp.float32))
        scaled = (jnp.exp(cum_k[:, -1:, :] - cum_k) * step_k)[..., None] * xs_k.astype(jnp.float32)
        scaled = widened(scaled.astype(jnp.bfloat16))
        b_heads = jnp.repeat(bs_k, per_group, axis=2).astype(jnp.float32)
        c_heads = jnp.repeat(cs_k, per_group, axis=2).astype(jnp.float32)
        update = jnp.einsum('suhp,suhn->shpn', scaled, b_heads)
        entry_low = widened(entry_state.astype(jnp.bfloat16))
        carried = jnp.exp(cum_k)[..., None] * jnp.einsum('sqhn,shpn->sqhp', c_heads, entry_low)
        ssm_block = intra_part + carried + skip_scale[None, None, :, None] * xs_k.astype(jnp.float32)
        following = jnp.exp(cum_k[:, -1, :])[:, :, None, None] * entry_state + update
        return (following, ssm_block)
    per_block = tuple((jnp.moveaxis(item_array, 1, 0) for item_array in (xs_all, bs_all, cs_all, step_size, cumulative)))
    start_state = jnp.zeros((BATCH_COUNT, HEADS, HEAD_DIM, STATE), jnp.float32)
    final_state, ssm_blocks = lax.scan(advance, start_state, per_block)
    ssm_out = jnp.moveaxis(ssm_blocks, 0, 1).reshape(BATCH_COUNT, CONTEXT_SPAN, INNER)
    gate_values = to_blocks(z_in).reshape(BATCH_COUNT, CONTEXT_SPAN, INNER).astype(jnp.float32)
    gated_out = ssm_out * sigmoid_gate(gate_values)
    grouped = gated_out.reshape(BATCH_COUNT, CONTEXT_SPAN, GROUPS, INNER // GROUPS)
    spread = lax.optimization_barrier(jnp.mean(grouped * grouped, axis=3, keepdims=True))
    normed = ((grouped * lax.rsqrt(spread + 1e-05)).reshape(BATCH_COUNT, CONTEXT_SPAN, INNER) * norm_gain).astype(jnp.bfloat16)
    flat_rows = normed.reshape(BATCH_COUNT * CONTEXT_SPAN, INNER)
    block_cols = INNER // N_HEAD
    running = jnp.zeros((BATCH_COUNT * CONTEXT_SPAN, D), jnp.float32)
    for block_index in range(N_HEAD):
        partial_value = jnp.dot(flat_rows[:, block_index * block_cols:(block_index + 1) * block_cols], out_weight[block_index * block_cols:(block_index + 1) * block_cols], preferred_element_type=jnp.float32)
        running = running + widened(partial_value.astype(jnp.bfloat16))
    result = running.astype(jnp.bfloat16).reshape(BATCH_COUNT, block_count, HALF, D)
    return from_blocks(result)
```

```python
import jax
import jax.numpy as jnp
from jax import lax
from jax.sharding import PartitionSpec as P

HEAD_DIM = 64
STATE = 128
KW = 4
HALF = 192


def shifted(block, axis, distance):
    devices = range(lax.axis_size(axis))
    route = [(i - distance, i) for i in devices if i - distance in devices]
    return lax.ppermute(block, axis, route)


def sigmoid_gate(values):
    return values / (1.0 + jnp.exp(-values))


def chain_entries(block_decay, update):
    size = lax.axis_size("ctx")
    seq_count, _, heads_here, rows, cols = update.shape
    owned = heads_here // size

    def spread(values):
        split = values.reshape((seq_count, 2, size, owned) + values.shape[3:])
        return lax.all_to_all(jnp.moveaxis(split, 2, 0), "ctx", 0, 0)

    decays = spread(block_decay)
    updates = spread(update.astype(jnp.bfloat16))
    order = [(c, 0) for c in range(size)] + [(c, 1) for c in reversed(range(size))]
    state = jnp.zeros((seq_count, owned, rows, cols), jnp.float32)
    entry = [[None, None] for _ in range(size)]
    for c, half in order:
        entry[c][half] = state.astype(jnp.bfloat16)
        state = decays[c, :, half][..., None, None] * state + updates[c, :, half].astype(
            jnp.float32
        )
    stacked = jnp.stack([jnp.stack(pair, axis=1) for pair in entry])
    back = lax.all_to_all(stacked, "ctx", 0, 0)
    return jnp.moveaxis(back, 0, 2).reshape(seq_count, 2, heads_here, rows, cols)


def mixer(
    x_part, z_part, bc_part, conv_x, conv_bc, dt_part, a_log, skip_scale, norm_gain, out_weight
):
    seq_count, tok_count, inner_cols = x_part.shape
    group_cols = bc_part.shape[3]
    heads_here = a_log.shape[0]
    groups_here = group_cols // STATE
    per_group = heads_here // groups_here
    block_count = 2 * seq_count
    lag_rows = KW - 1
    joined = jnp.concatenate(
        [x_part, bc_part.reshape(seq_count, tok_count, 2 * group_cols)], axis=2
    )
    halves = joined.reshape(seq_count, 2, HALF, joined.shape[2])
    tail_rows = halves[:, :, HALF - lag_rows :]
    from_lower = shifted(tail_rows[:, 0], "ctx", 1)
    from_upper = shifted(tail_rows[:, 1], "ctx", -1)
    last_flag = lax.axis_index("ctx") == lax.axis_size("ctx") - 1
    upper_lead = jnp.where(last_flag, tail_rows[:, 0], from_upper)
    padded = jnp.concatenate([jnp.stack([from_lower, upper_lead], axis=1), halves], axis=2)
    conv_taps = jnp.concatenate([conv_x, conv_bc.reshape(KW, 2 * group_cols)], axis=1)
    summed = jnp.zeros(halves.shape, jnp.float32)
    for tap_index in range(KW):
        summed = summed + conv_taps[tap_index] * padded[:, :, tap_index : tap_index + HALF].astype(
            jnp.float32
        )
    conv_out = sigmoid_gate(summed).astype(jnp.bfloat16)
    xs_all = conv_out[..., :inner_cols].reshape(block_count, HALF, heads_here, HEAD_DIM)
    bs_all = conv_out[..., inner_cols : inner_cols + group_cols].reshape(
        block_count, HALF, groups_here, STATE
    )
    cs_all = conv_out[..., inner_cols + group_cols :].reshape(block_count, HALF, groups_here, STATE)
    step_size = (
        jax.nn.softplus(dt_part)
        .reshape(seq_count, heads_here, 2, HALF)
        .transpose(0, 2, 1, 3)
        .reshape(block_count, heads_here, HALF)
    )
    cumulative = jnp.cumsum(step_size * (-jnp.exp(a_log))[None, :, None], axis=2)
    causal = jnp.tril(jnp.ones((HALF, HALF), dtype=bool))
    scores = jnp.einsum("bqgn,bugn->bgqu", cs_all, bs_all, preferred_element_type=jnp.float32)
    gap_matrix = cumulative[:, :, :, None] - cumulative[:, :, None, :]
    factor = jnp.where(causal, jnp.exp(jnp.where(causal, gap_matrix, 0.0)), 0.0)
    factor = factor.reshape(block_count, groups_here, per_group, HALF, HALF)
    step_cols = step_size.reshape(block_count, groups_here, per_group, 1, HALF)
    weights = (
        (scores[:, :, None] * factor * step_cols)
        .reshape(block_count, heads_here, HALF, HALF)
        .astype(jnp.bfloat16)
    )
    intra_part = jnp.einsum("bhqu,buhp->bqhp", weights, xs_all, preferred_element_type=jnp.float32)
    tail_decay = jnp.exp(cumulative[:, :, -1:] - cumulative) * step_size
    scaled = (tail_decay.transpose(0, 2, 1)[..., None] * xs_all).astype(jnp.bfloat16)
    update = jnp.einsum(
        "bugkp,bugn->bgkpn",
        scaled.reshape(block_count, HALF, groups_here, per_group, HEAD_DIM),
        bs_all,
        preferred_element_type=jnp.float32,
    )
    update = update.reshape(block_count, heads_here, HEAD_DIM, STATE)
    block_decay = jnp.exp(cumulative[:, :, -1])
    entries = chain_entries(
        block_decay.reshape(seq_count, 2, heads_here),
        update.reshape(seq_count, 2, heads_here, HEAD_DIM, STATE),
    )
    entry_low = entries.reshape(block_count, groups_here, per_group, HEAD_DIM, STATE).astype(
        jnp.bfloat16
    )
    carried = jnp.einsum(
        "bqgn,bgkpn->bqgkp", cs_all, entry_low, preferred_element_type=jnp.float32
    ).reshape(block_count, HALF, heads_here, HEAD_DIM)
    carried = jnp.exp(cumulative).transpose(0, 2, 1)[..., None] * carried
    ssm_out = intra_part + carried + skip_scale[None, None, :, None] * xs_all
    gated_out = ssm_out.reshape(seq_count, tok_count, inner_cols) * sigmoid_gate(
        z_part.astype(jnp.float32)
    )
    grouped = gated_out.reshape(seq_count, tok_count, groups_here, inner_cols // groups_here)
    spread = jnp.mean(grouped * grouped, axis=3, keepdims=True)
    normed = (
        (grouped * lax.rsqrt(spread + 1e-05)).reshape(seq_count * tok_count, inner_cols) * norm_gain
    ).astype(jnp.bfloat16)
    summed_out = lax.psum_scatter(
        lax.dot_general(
            out_weight, normed, (((0,), (1,)), ((), ())), preferred_element_type=jnp.float32
        ).astype(jnp.bfloat16),
        "head",
        scatter_dimension=0,
        tiled=True,
    ).astype(jnp.float32)
    return summed_out.T.reshape(seq_count, tok_count, summed_out.shape[0]).astype(jnp.bfloat16)


def body(x_in, z_in, bc_in, conv_x, conv_bc, dt_raw, a_log, skip_scale, norm_gain, out_weight):
    return mixer(
        x_in, z_in, bc_in, conv_x, conv_bc, dt_raw, a_log, skip_scale, norm_gain, out_weight
    )


def solution(mesh):
    in_specs = (
        P(None, "ctx", "head"),
        P(None, "ctx", "head"),
        P(None, "ctx", None, "head"),
        P(None, "head"),
        P(None, None, "head"),
        P(None, "head", "ctx"),
        P("head"),
        P("head"),
        P("head"),
        P("head", None),
    )
    out_specs = P(None, "ctx", "head")
    return jax.shard_map(body, mesh=mesh, in_specs=in_specs, out_specs=out_specs, check_vma=False)
```

```python
import jax
import jax.numpy as jnp
from jax import lax
from jax.experimental import pallas as pl
from jax.experimental.pallas import tpu as pltpu
from jax.sharding import PartitionSpec as P

HEAD_DIM = 64
STATE = 128
KW = 4
HALF = 192
MESH = pl.DeviceIdType.MESH
REACH = (2, 1, 3, 0)


def place():
    c, h = lax.axis_index("ctx"), lax.axis_index("head")
    return c // 4, (c // 2) % 2, c % 2, h // 2, h % 2


def device(z, y_lo, core, x, y_hi):
    return (z * 4 + y_lo * 2 + core, x * 2 + y_hi)


def greet(devices):
    barrier = pltpu.get_barrier_semaphore()
    for one in devices:
        pl.semaphore_signal(barrier, inc=1, device_id=one, device_id_type=MESH)
    pl.semaphore_wait(barrier, len(devices))


def remote(src, dst, send_sem, recv_sem, target):
    return pltpu.make_async_remote_copy(
        src_ref=src,
        dst_ref=dst,
        send_sem=send_sem,
        recv_sem=recv_sem,
        device_id=target,
        device_id_type=MESH,
    )


def weight_kernel(w_ref, wr_ref, in_s, in_r, z_s, z_r, far_s, far_r, core_s, core_r):
    z, y_lo, core, x, y_hi = place()
    partner = device(z, 1 - y_lo, core, x, 1 - y_hi)
    up = device((z + 1) % 4, y_lo, core, x, y_hi)
    down = device((z + 3) % 4, y_lo, core, x, y_hi)
    other = device(z, y_lo, 1 - core, x, y_hi)
    depth, cols = wr_ref.shape[1:]
    part = depth // 8

    def rows(step, which):
        return pl.ds(pl.multiple_of((((z + step) % 4) * 2 + which) * part, part), part)

    greet([partner, up, down, other])
    mine = rows(0, core)
    started = []

    def start(copy):
        copy.start()
        started.append(copy)
        return copy

    def pair(g, step, send_sem, recv_sem, target):
        here = wr_ref.at[pl.ds(2 * g, 2), rows(step, core)]
        return remote(here, here, send_sem, recv_sem, target)

    ins = []
    for d in range(4):
        block = 2 * ((x + REACH[d]) % 4) + 1 - y_hi
        src = w_ref.at[mine, pl.ds(pl.multiple_of(block * cols, cols), cols)]
        ins.append(start(remote(src, wr_ref.at[d, mine], in_s.at[d], in_r.at[d], partner)))
    near, across = {}, []
    for g in range(2):
        ins[2 * g].wait_recv()
        ins[2 * g + 1].wait_recv()
        near[g, 0] = start(pair(g, 0, z_s.at[g, 0], z_r.at[g, 0], up))
        near[g, 1] = start(pair(g, 0, z_s.at[g, 1], z_r.at[g, 1], down))
        across.append(start(pair(g, 0, core_s.at[g, 0], core_r.at[g, 0], other)))
    far = {}
    for g in range(2):
        for way in range(2):
            near[g, way].wait_recv()
            step = 3 if way == 0 else 1
            half = wr_ref.at[2 * g + way, rows(step, core)]
            far[g, way] = start(
                remote(
                    half, half, far_s.at[g, way], far_r.at[g, way], up if way == 0 else down
                )
            )
            across.append(
                start(pair(g, step, core_s.at[g, 1 + way], core_r.at[g, 1 + way], other))
            )
    for g in range(2):
        far[g, 0].wait_recv()
        far[g, 1].wait_recv()
        across.append(start(pair(g, 2, core_s.at[g, 3], core_r.at[g, 3], other)))
    for copy in across:
        copy.wait_recv()
    for copy in started:
        copy.wait_send()


def exchange_weights(out_weight):
    depth, width = out_weight.shape
    dma = pltpu.SemaphoreType.DMA
    return pl.pallas_call(
        weight_kernel,
        out_shape=jax.ShapeDtypeStruct((4, depth, width // 8), out_weight.dtype),
        in_specs=[pl.BlockSpec(memory_space=pl.ANY)],
        out_specs=pl.BlockSpec(memory_space=pl.ANY),
        scratch_shapes=[
            dma((4,)), dma((4,)), dma((2, 2)), dma((2, 2)), dma((2, 2)), dma((2, 2)),
            dma((2, 4)), dma((2, 4)),
        ],
        compiler_params=pltpu.CompilerParams(collective_id=1, has_side_effects=True),
        name="weight_exchange",
    )(out_weight)


def project_kernel(
    n_ref, w_ref, wr_ref, out_ref,
    act, wts, mid, keep, direct, joined, own, relay, final,
    load_s, act_s, y_s, y_r, mid_s, mid_r, fin_s, fin_r,
):
    z, y_lo, core, x, y_hi = place()
    partner = device(z, y_lo, core, x, 1 - y_hi)
    right = device(z, y_lo, core, (x + 1) % 4, y_hi)
    left = device(z, y_lo, core, (x + 3) % 4, y_hi)
    ways = (right, left)
    tokens, depth = n_ref.shape
    cols = out_ref.shape[1]
    half = cols // 2
    tiles = tokens // HALF

    def rows(t):
        return pl.ds(pl.multiple_of(t * HALF, HALF), HALF)

    def loads(d):
        block = 2 * ((x + REACH[d]) % 4) + y_hi
        src = w_ref.at[:, pl.ds(pl.multiple_of(block * cols, cols), cols)]
        return (
            pltpu.make_async_copy(src, wts.at[d, pl.ds(0, depth)], load_s.at[d, 0]),
            pltpu.make_async_copy(wr_ref.at[d], wts.at[d, pl.ds(depth, depth)], load_s.at[d, 1]),
        )

    own_act = pltpu.make_async_copy(n_ref, act.at[:, pl.ds(0, depth)], act_s)

    def to_partner(t):
        return remote(
            n_ref.at[rows(t)], act.at[rows(t), pl.ds(depth, depth)], y_s.at[t], y_r.at[t], partner
        )

    def pass_on(t, way):
        return remote(
            mid.at[way, rows(t)], relay.at[way, rows(t)], mid_s.at[t, way], mid_r.at[t, way],
            ways[way],
        )

    def send_direct(t, way):
        return remote(
            direct.at[way, rows(t)], final.at[way, 0, rows(t)], fin_s.at[t, way, 0],
            fin_r.at[t, way, 0], ways[way],
        )

    def send_joined(t, way):
        return remote(
            joined.at[way, rows(t)], final.at[way, 1, rows(t)], fin_s.at[t, way, 1],
            fin_r.at[t, way, 1], ways[way],
        )

    own_act.start()
    for d in range(4):
        for copy in loads(d):
            copy.start()
    greet([partner, right, left])
    for t in range(tiles):
        to_partner(t).start()
    own_act.wait()

    def product(t, d, side):
        return jnp.dot(
            act[rows(t)], wts[d, :, side * half : (side + 1) * half],
            preferred_element_type=jnp.float32,
        )

    def ready(t, d):
        @pl.when(t == 0)
        def _():
            for copy in loads(d):
                copy.wait()

    def finish(t):
        for way in range(2):
            send_direct(t, way).wait_recv()
            send_joined(t, way).wait_recv()
        r = rows(t)
        for side in range(2):
            total = own[r, side * half : (side + 1) * half]
            total = total + final[0, 1 - side, r].astype(jnp.float32)
            total = total + final[1, side, r].astype(jnp.float32)
            out_ref[r, side * half : (side + 1) * half] = total.astype(out_ref.dtype)

    def tile(t, carry):
        r = rows(t)
        to_partner(t).wait_recv()
        ready(t, 0)
        for way in range(2):
            mid[way, r] = product(t, 0, way).astype(mid.dtype)
            pass_on(t, way).start()
        for way in range(2):
            ready(t, 1 + way)
            direct[way, r] = product(t, 1 + way, 1 - way).astype(direct.dtype)
            send_direct(t, way).start()
            keep[way, r] = product(t, 1 + way, way)
        ready(t, 3)
        for side in range(2):
            own[r, side * half : (side + 1) * half] = product(t, 3, side)
        for way in range(2):
            pass_on(t, way).wait_recv()
            joined[way, r] = (keep[way, r] + relay[way, r].astype(jnp.float32)).astype(joined.dtype)
            send_joined(t, way).start()

        @pl.when(t > 0)
        def _():
            finish(t - 1)

        return carry

    lax.fori_loop(0, tiles, tile, 0)
    finish(tiles - 1)

    def drain(t, carry):
        to_partner(t).wait_send()
        for way in range(2):
            pass_on(t, way).wait_send()
            send_direct(t, way).wait_send()
            send_joined(t, way).wait_send()
        return carry

    lax.fori_loop(0, tiles, drain, 0)


def project(normed, out_weight, received):
    tokens, depth = normed.shape
    cols = out_weight.shape[1] // 8
    half = cols // 2
    tiles = tokens // HALF
    dma = pltpu.SemaphoreType.DMA
    low, wide = jnp.bfloat16, jnp.float32
    return pl.pallas_call(
        project_kernel,
        out_shape=jax.ShapeDtypeStruct((tokens, cols), low),
        in_specs=[
            pl.BlockSpec(memory_space=pltpu.VMEM),
            pl.BlockSpec(memory_space=pl.ANY),
            pl.BlockSpec(memory_space=pl.ANY),
        ],
        out_specs=pl.BlockSpec(memory_space=pltpu.VMEM),
        scratch_shapes=[
            pltpu.VMEM((tokens, 2 * depth), low),
            pltpu.VMEM((4, 2 * depth, cols), low),
            pltpu.VMEM((2, tokens, half), low),
            pltpu.VMEM((2, tokens, half), wide),
            pltpu.VMEM((2, tokens, half), low),
            pltpu.VMEM((2, tokens, half), low),
            pltpu.VMEM((tokens, cols), wide),
            pltpu.VMEM((2, tokens, half), low),
            pltpu.VMEM((2, 2, tokens, half), low),
            dma((4, 2)), dma, dma((tiles,)), dma((tiles,)), dma((tiles, 2)), dma((tiles, 2)),
            dma((tiles, 2, 2)), dma((tiles, 2, 2)),
        ],
        compiler_params=pltpu.CompilerParams(
            collective_id=2, has_side_effects=True, vmem_limit_bytes=56 << 20
        ),
        name="projection",
    )(normed, out_weight, received)


def shifted(block, axis, distance):
    devices = range(lax.axis_size(axis))
    route = [(i - distance, i) for i in devices if i - distance in devices]
    return lax.ppermute(block, axis, route)


def sigmoid_gate(values):
    return values / (1.0 + jnp.exp(-values))


def chain_entries(block_decay, update):
    size = lax.axis_size("ctx")
    seq_count, _, heads_here, rows, cols = update.shape
    owned = heads_here // size

    def spread(values):
        split = values.reshape((seq_count, 2, size, owned) + values.shape[3:])
        return lax.all_to_all(jnp.moveaxis(split, 2, 0), "ctx", 0, 0)

    decays = spread(block_decay)
    updates = spread(update.astype(jnp.bfloat16))
    order = [(c, 0) for c in range(size)] + [(c, 1) for c in reversed(range(size))]
    state = jnp.zeros((seq_count, owned, rows, cols), jnp.float32)
    entry = [[None, None] for _ in range(size)]
    for c, half in order:
        entry[c][half] = state.astype(jnp.bfloat16)
        state = decays[c, :, half][..., None, None] * state + updates[c, :, half].astype(
            jnp.float32
        )
    stacked = jnp.stack([jnp.stack(pair, axis=1) for pair in entry])
    back = lax.all_to_all(stacked, "ctx", 0, 0)
    return jnp.moveaxis(back, 0, 2).reshape(seq_count, 2, heads_here, rows, cols)


def mixer(
    x_part, z_part, bc_part, conv_x, conv_bc, dt_part, a_log, skip_scale, norm_gain, out_weight
):
    seq_count, tok_count, inner_cols = x_part.shape
    group_cols = bc_part.shape[3]
    heads_here = a_log.shape[0]
    groups_here = group_cols // STATE
    per_group = heads_here // groups_here
    block_count = 2 * seq_count
    lag_rows = KW - 1
    joined = jnp.concatenate(
        [x_part, bc_part.reshape(seq_count, tok_count, 2 * group_cols)], axis=2
    )
    halves = joined.reshape(seq_count, 2, HALF, joined.shape[2])
    tail_rows = halves[:, :, HALF - lag_rows :]
    from_lower = shifted(tail_rows[:, 0], "ctx", 1)
    from_upper = shifted(tail_rows[:, 1], "ctx", -1)
    last_flag = lax.axis_index("ctx") == lax.axis_size("ctx") - 1
    upper_lead = jnp.where(last_flag, tail_rows[:, 0], from_upper)
    padded = jnp.concatenate([jnp.stack([from_lower, upper_lead], axis=1), halves], axis=2)
    conv_taps = jnp.concatenate([conv_x, conv_bc.reshape(KW, 2 * group_cols)], axis=1)
    summed = jnp.zeros(halves.shape, jnp.float32)
    for tap_index in range(KW):
        summed = summed + conv_taps[tap_index] * padded[:, :, tap_index : tap_index + HALF].astype(
            jnp.float32
        )
    conv_out = sigmoid_gate(summed).astype(jnp.bfloat16)
    xs_all = conv_out[..., :inner_cols].reshape(block_count, HALF, heads_here, HEAD_DIM)
    bs_all = conv_out[..., inner_cols : inner_cols + group_cols].reshape(
        block_count, HALF, groups_here, STATE
    )
    cs_all = conv_out[..., inner_cols + group_cols :].reshape(block_count, HALF, groups_here, STATE)
    step_size = (
        jax.nn.softplus(dt_part)
        .reshape(seq_count, heads_here, 2, HALF)
        .transpose(0, 2, 1, 3)
        .reshape(block_count, heads_here, HALF)
    )
    cumulative = jnp.cumsum(step_size * (-jnp.exp(a_log))[None, :, None], axis=2)
    causal = jnp.tril(jnp.ones((HALF, HALF), dtype=bool))
    scores = jnp.einsum("bqgn,bugn->bgqu", cs_all, bs_all, preferred_element_type=jnp.float32)
    gap_matrix = cumulative[:, :, :, None] - cumulative[:, :, None, :]
    factor = jnp.where(causal, jnp.exp(jnp.where(causal, gap_matrix, 0.0)), 0.0)
    factor = factor.reshape(block_count, groups_here, per_group, HALF, HALF)
    step_cols = step_size.reshape(block_count, groups_here, per_group, 1, HALF)
    weights = (
        (scores[:, :, None] * factor * step_cols)
        .reshape(block_count, heads_here, HALF, HALF)
        .astype(jnp.bfloat16)
    )
    intra_part = jnp.einsum("bhqu,buhp->bqhp", weights, xs_all, preferred_element_type=jnp.float32)
    tail_decay = jnp.exp(cumulative[:, :, -1:] - cumulative) * step_size
    scaled = (tail_decay.transpose(0, 2, 1)[..., None] * xs_all).astype(jnp.bfloat16)
    update = jnp.einsum(
        "bugkp,bugn->bgkpn",
        scaled.reshape(block_count, HALF, groups_here, per_group, HEAD_DIM),
        bs_all,
        preferred_element_type=jnp.float32,
    )
    update = update.reshape(block_count, heads_here, HEAD_DIM, STATE)
    block_decay = jnp.exp(cumulative[:, :, -1])
    entries = chain_entries(
        block_decay.reshape(seq_count, 2, heads_here),
        update.reshape(seq_count, 2, heads_here, HEAD_DIM, STATE),
    )
    entry_low = entries.reshape(block_count, groups_here, per_group, HEAD_DIM, STATE).astype(
        jnp.bfloat16
    )
    carried = jnp.einsum(
        "bqgn,bgkpn->bqgkp", cs_all, entry_low, preferred_element_type=jnp.float32
    ).reshape(block_count, HALF, heads_here, HEAD_DIM)
    carried = jnp.exp(cumulative).transpose(0, 2, 1)[..., None] * carried
    ssm_out = intra_part + carried + skip_scale[None, None, :, None] * xs_all
    gated_out = ssm_out.reshape(seq_count, tok_count, inner_cols) * sigmoid_gate(
        z_part.astype(jnp.float32)
    )
    grouped = gated_out.reshape(seq_count, tok_count, groups_here, inner_cols // groups_here)
    spread = jnp.mean(grouped * grouped, axis=3, keepdims=True)
    normed = (
        (grouped * lax.rsqrt(spread + 1e-05)).reshape(seq_count * tok_count, inner_cols) * norm_gain
    ).astype(jnp.bfloat16)
    projected = project(normed, out_weight, exchange_weights(out_weight))
    return projected.reshape(seq_count, tok_count, projected.shape[1])


def body(x_in, z_in, bc_in, conv_x, conv_bc, dt_raw, a_log, skip_scale, norm_gain, out_weight):
    return mixer(
        x_in, z_in, bc_in, conv_x, conv_bc, dt_raw, a_log, skip_scale, norm_gain, out_weight
    )


def solution(mesh):
    in_specs = (
        P(None, "ctx", "head"),
        P(None, "ctx", "head"),
        P(None, "ctx", None, "head"),
        P(None, "head"),
        P(None, None, "head"),
        P(None, "head", "ctx"),
        P("head"),
        P("head"),
        P("head"),
        P("head", None),
    )
    out_specs = P(None, "ctx", "head")
    return jax.shard_map(body, mesh=mesh, in_specs=in_specs, out_specs=out_specs, check_vma=False)
```

```python
import jax
import jax.numpy as jnp
from jax import lax
from jax.experimental import pallas as pl
from jax.experimental.pallas import tpu as pltpu
from jax.sharding import PartitionSpec as P

HEAD_DIM = 64
STATE = 128
KW = 4
HALF = 192
MESH = pl.DeviceIdType.MESH
REACH = (2, 1, 3, 0)


def place():
    c, h = lax.axis_index("ctx"), lax.axis_index("head")
    return c // 4, (c // 2) % 2, c % 2, h // 2, h % 2


def device(z, y_lo, core, x, y_hi):
    return (z * 4 + y_lo * 2 + core, x * 2 + y_hi)


def greet(devices):
    barrier = pltpu.get_barrier_semaphore()
    for one in devices:
        pl.semaphore_signal(barrier, inc=1, device_id=one, device_id_type=MESH)
    pl.semaphore_wait(barrier, len(devices))


def remote(src, dst, send_sem, recv_sem, target):
    return pltpu.make_async_remote_copy(
        src_ref=src,
        dst_ref=dst,
        send_sem=send_sem,
        recv_sem=recv_sem,
        device_id=target,
        device_id_type=MESH,
    )


def rounded_parts(values):
    high = values.astype(jnp.bfloat16)
    rest = values - high.astype(jnp.float32)
    middle = rest.astype(jnp.bfloat16)
    low = (rest - middle.astype(jnp.float32)).astype(jnp.bfloat16)
    return jnp.concatenate([high, middle, low], axis=0)


def unit(size):
    rows = lax.broadcasted_iota(jnp.int32, (size, size), 0)
    cols = lax.broadcasted_iota(jnp.int32, (size, size), 1)
    return jnp.where(rows == cols, 1.0, 0.0).astype(jnp.bfloat16)


def by_rows(left, right):
    return lax.dot_general(
        left, right, (((1,), (1,)), ((), ())), preferred_element_type=jnp.float32
    )


def mixer_kernel(
    x_ref, bc_ref, dt_ref, a_ref, skip_ref, gain_ref, taps_ref, taps_bc_ref, z_ref, w_ref,
    n_ref, wr_ref,
    halo_x, halo_bc, wide, xs, bs, cs, cum_row, dt_row, cum_col, tail3, cum3, spread3,
    scaled, upd, got, back, ent, dec, decs, steps, inner, zbuf,
    z_sem, halo_s, halo_r, dec_s, dec_r, own_s, upd_s, upd_r, ent_s, ent_r,
    in_s, in_r, z_s, z_r, far_s, far_r, core_s, core_r,
):
    f32, bf16 = jnp.float32, jnp.bfloat16
    z, y_lo, core, x, y_hi = place()
    me = lax.axis_index("ctx")
    head = lax.axis_index("head")
    cols = x_ref.shape[3]
    state_rows, lanes = got.shape[2:]
    heads = dt_ref.shape[1]

    partner = device(z, 1 - y_lo, core, x, 1 - y_hi)
    up = device((z + 1) % 4, y_lo, core, x, y_hi)
    down = device((z + 3) % 4, y_lo, core, x, y_hi)
    other = device(z, y_lo, 1 - core, x, y_hi)
    depth = wr_ref.shape[1]
    part = depth // 8

    def part_rows(step):
        return pl.ds(pl.multiple_of((((z + step) % 4) * 2 + core) * part, part), part)

    def import_part(d):
        block = 2 * ((x + REACH[d]) % 4) + 1 - y_hi
        src = w_ref.at[part_rows(0), pl.ds(pl.multiple_of(block * cols, cols), cols)]
        return remote(src, wr_ref.at[d, part_rows(0)], in_s.at[d], in_r.at[d], partner)

    def near(g, way):
        here = wr_ref.at[pl.ds(2 * g, 2), part_rows(0)]
        return remote(here, here, z_s.at[g, way], z_r.at[g, way], down if way else up)

    def far(g, way):
        here = wr_ref.at[2 * g + way, part_rows(1 if way else 3)]
        return remote(here, here, far_s.at[g, way], far_r.at[g, way], down if way else up)

    def across(g, step):
        here = wr_ref.at[pl.ds(2 * g, 2), part_rows(step)]
        return remote(here, here, core_s.at[g, step], core_r.at[g, step], other)

    def weights_first(g):
        import_part(2 * g).wait_recv()
        import_part(2 * g + 1).wait_recv()
        near(g, 0).start()
        near(g, 1).start()
        across(g, 0).start()

    def weights_second(g):
        for way in range(2):
            near(g, way).wait_recv()
            far(g, way).start()
            across(g, 1 if way else 3).start()

    def weights_third(g):
        far(g, 0).wait_recv()
        far(g, 1).wait_recv()
        across(g, 2).start()

    def weights_end():
        for g in range(2):
            for step in range(4):
                across(g, step).wait_recv()
        for d in range(4):
            import_part(d).wait_send()
        for g in range(2):
            for way in range(2):
                near(g, way).wait_send()
                far(g, way).wait_send()
            for step in range(4):
                across(g, step).wait_send()

    def peer(step):
        return (me + step) % 16

    def at(index):
        return (index, head)

    def halo(half):
        target = at(peer(15 if half else 1))
        rows = pl.ds(HALF - 16, 16)
        return (
            remote(
                x_ref.at[:, half, rows], halo_x.at[half], halo_s.at[half, 0], halo_r.at[half, 0],
                target,
            ),
            remote(
                bc_ref.at[:, half, rows], halo_bc.at[half], halo_s.at[half, 1],
                halo_r.at[half, 1], target,
            ),
        )

    def share(ref, s, owner):
        return ref.at[
            pl.ds(2 * s, 2),
            pl.ds(pl.multiple_of((owner // 2) * state_rows, state_rows), state_rows),
            pl.ds(pl.multiple_of((owner % 2) * lanes, lanes), lanes),
        ]

    def send_decay(step):
        return remote(dec, decs.at[me], dec_s.at[step], dec_r.at[step], at(peer(step)))

    def send_update(s, step):
        owner = peer(step)
        return remote(
            share(upd, s, owner), got.at[me, pl.ds(2 * s, 2)], upd_s.at[s, step],
            upd_r.at[s, step], at(owner),
        )

    def send_entry(s, step):
        target = peer(step)
        return remote(
            back.at[target, pl.ds(2 * s, 2)], share(ent, s, me), ent_s.at[s, step],
            ent_r.at[s, step], at(target),
        )

    def keep_update(s):
        return pltpu.make_async_copy(share(upd, s, me), got.at[me, pl.ds(2 * s, 2)], own_s.at[s])

    def keep_entry(s):
        return pltpu.make_async_copy(back.at[me, pl.ds(2 * s, 2)], share(ent, s, me), own_s.at[s])

    def each_peer(work):
        def step(i, carry):
            work(i)
            return carry

        lax.fori_loop(1, 16, step, 0)

    z_copy = pltpu.make_async_copy(z_ref, zbuf, z_sem)
    z_copy.start()
    barrier = pltpu.get_barrier_semaphore()

    def hello(i):
        pl.semaphore_signal(barrier, inc=1, device_id=at(peer(i)), device_id_type=MESH)

    each_peer(hello)
    pl.semaphore_signal(barrier, inc=1, device_id=partner, device_id_type=MESH)
    pl.semaphore_wait(barrier, 16)
    for half in range(2):
        for copy in halo(half):
            copy.start()
    for d in range(4):
        import_part(d).start()

    row_id = lax.broadcasted_iota(jnp.int32, (HALF, HALF), 0)
    col_id = lax.broadcasted_iota(jnp.int32, (HALF, HALF), 1)
    causal = row_id >= col_id
    eye = unit(HALF)
    ahead = jnp.where(row_id <= col_id, 1.0, 0.0).astype(bf16)
    rate = -jnp.exp(a_ref[...])
    dec[...] = jnp.zeros_like(dec)
    for b in range(4):
        raw = dt_ref[b]
        step_size = jnp.maximum(raw, 0.0) + jnp.log1p(jnp.exp(-jnp.abs(raw)))
        fall = rounded_parts(step_size * rate)
        sums = jnp.dot(fall, ahead, preferred_element_type=f32)
        cum = sums[:heads] + sums[heads : 2 * heads] + sums[2 * heads :]
        dt_row[b] = step_size
        cum_row[b] = cum
        turned = by_rows(eye, rounded_parts(cum))
        col = turned[:, :heads] + turned[:, heads : 2 * heads] + turned[:, 2 * heads :]
        cum_col[b] = col
        dec[b : b + 1, :heads] = jnp.exp(col[HALF - 1 :])
        tail = jnp.exp(cum[:, HALF - 1 :] - cum) * step_size
        tail3[b] = by_rows(eye, rounded_parts(tail)).astype(bf16)
        cum3[b] = by_rows(eye, rounded_parts(jnp.exp(cum))).astype(bf16)
    of_head = lax.broadcasted_iota(jnp.int32, spread3.shape, 1) // HEAD_DIM
    of_part = lax.broadcasted_iota(jnp.int32, spread3.shape, 0) % heads
    spread3[...] = jnp.where(of_head == of_part, 1.0, 0.0).astype(bf16)
    each_peer(lambda i: send_decay(i).start())
    decs[me] = dec[...]
    for half in range(2):
        for copy in halo(half):
            copy.wait_recv()

    turn = unit(STATE)
    chunk = 256
    band = 64

    def convolve(s, half, start, width, src, lead_ref, taps, put):
        before = lead_ref[0, s, :, pl.ds(start, width)]
        before = jnp.where(me == 0, jnp.zeros_like(before), before)
        turned = jnp.where(
            me == 15, src[s, 0, HALF - 16 :, pl.ds(start, width)],
            lead_ref[1, s, :, pl.ds(start, width)],
        )
        lead = jnp.where(half == 0, before, turned)
        wide[0:8] = lead.astype(f32)[8:]
        wide[8:] = src[s, half, :, pl.ds(start, width)].astype(f32)
        tap = taps[:, pl.ds(start, width)]
        for r in range(0, HALF, band):
            total = tap[0:1] * wide[r + 5 : r + 5 + band]
            for k in range(1, KW):
                total = total + tap[k : k + 1] * wide[r + 5 + k : r + 5 + k + band]
            put(r, (total / (1.0 + jnp.exp(-total))).astype(bf16))

    def front(b, carry):
        s, half = b // 2, b % 2

        def put_bc(r, values):
            bs[b, r : r + band] = values[:, :STATE]
            cs[b, r : r + band] = values[:, STATE:]

        convolve(s, half, 0, chunk, bc_ref, halo_bc, taps_bc_ref, put_bc)
        bs_turned = by_rows(turn, bs[b]).astype(bf16)

        def columns(i, carry):
            start = pl.multiple_of(i * chunk, chunk)

            def put(r, values):
                xs[b, r : r + band, pl.ds(start, chunk)] = values

            convolve(s, half, start, chunk, x_ref, halo_x, taps_ref, put)
            for r in range(0, HALF, band):
                factor = jnp.dot(
                    tail3[b, r : r + band], spread3[:, pl.ds(start, chunk)],
                    preferred_element_type=f32,
                )
                scaled[r : r + band] = (
                    factor * xs[b, r : r + band, pl.ds(start, chunk)].astype(f32)
                ).astype(bf16)
            upd[b, :, pl.ds(start, chunk)] = jnp.dot(
                bs_turned, scaled[...], preferred_element_type=f32
            ).astype(bf16)
            return carry

        lax.fori_loop(0, cols // chunk, columns, 0)

        @pl.when(half == 1)
        def _():
            each_peer(lambda i: send_update(s, i).start())
            keep_update(s).start()

        return carry

    lax.fori_loop(0, 4, front, 0)

    first = 128

    def intra(b, carry):
        scores = jnp.where(causal, by_rows(cs[b], bs[b]), 0.0)
        low_half = lax.broadcasted_iota(jnp.int32, (1, 128), 1) < HEAD_DIM
        for p in range(heads // 2):
            tops, ends = [], []
            for h in (2 * p, 2 * p + 1):
                col = cum_col[b, :, h : h + 1]
                row = cum_row[b, h : h + 1]
                size = dt_row[b, h : h + 1]
                gap = jnp.minimum(col[:first] - row[:, :first], 0.0)
                tops.append(
                    (scores[:first, :first] * jnp.exp(gap) * size[:, :first]).astype(bf16)
                )
                gap = jnp.minimum(col[first:] - row, 0.0)
                ends.append((scores[first:] * jnp.exp(gap) * size).astype(bf16))
            pair = slice(128 * p, 128 * p + 128)
            top = jnp.dot(
                jnp.concatenate(tops, axis=0), xs[b, :first, pair], preferred_element_type=f32
            )
            end = jnp.dot(
                jnp.concatenate(ends, axis=0), xs[b, :, pair], preferred_element_type=f32
            )
            inner[b, :first, pair] = jnp.where(low_half, top[:first], top[first:])
            rest = HALF - first
            inner[b, first:, pair] = jnp.where(low_half, end[:rest], end[rest:])
        return carry

    def chain(s):
        each_peer(lambda i: send_update(s, i).wait_recv())
        keep_update(s).wait()
        state = jnp.zeros((state_rows, lanes), f32)
        for i in range(32):
            c, half = (i, 0) if i < 16 else (31 - i, 1)
            b = 2 * s + half
            back[c, b] = state.astype(bf16)
            state = steps[8 * c + b : 8 * c + b + 1] * state + got[c, b].astype(f32)
        each_peer(lambda i: send_entry(s, i).start())
        keep_entry(s).start()

    def finish(b, carry):
        squares = [jnp.zeros((96, 128), f32)] * 2
        for q in range(cols // chunk):
            part_cols = slice(q * chunk, (q + 1) * chunk)
            for i in range(2):
                r = slice(96 * i, 96 * i + 96)
                carried = jnp.dot(cs[b, r], ent[b, :, part_cols], preferred_element_type=f32)
                factor = jnp.dot(cum3[b, r], spread3[:, part_cols], preferred_element_type=f32)
                total = inner[b, r, part_cols] + factor * carried
                total = total + skip_ref[:, part_cols] * xs[b, r, part_cols].astype(f32)
                gate = zbuf[b, r, part_cols].astype(f32)
                total = total * (gate / (1.0 + jnp.exp(-gate)))
                inner[b, r, part_cols] = total
                square = total * total
                squares[i] = squares[i] + square[:, :128] + square[:, 128:]
        for i in range(2):
            spread = jnp.sum(squares[i], axis=1, keepdims=True) * (1.0 / cols)
            scale = lax.rsqrt(spread + 1e-05)
            r = slice(96 * i, 96 * i + 96)
            for q in range(cols // chunk):
                part_cols = slice(q * chunk, (q + 1) * chunk)
                n_ref[b, r, part_cols] = (
                    inner[b, r, part_cols] * scale * gain_ref[:, part_cols]
                ).astype(bf16)
        return carry

    def enter(s):
        each_peer(lambda i: send_entry(s, i).wait_recv())
        keep_entry(s).wait()

    weights_first(0)
    lax.fori_loop(0, 2, intra, 0)
    each_peer(lambda i: send_decay(i).wait_recv())
    head_id = lax.broadcasted_iota(jnp.int32, (128, lanes), 0)
    lane_head = lax.broadcasted_iota(jnp.int32, (128, lanes), 1) // HEAD_DIM
    picks = jnp.where(head_id == lane_head + (me % 2) * (lanes // HEAD_DIM), 1.0, 0.0).astype(bf16)
    stacked = rounded_parts(decs[...].reshape(128, 128))
    parts = jnp.dot(stacked, picks, preferred_element_type=f32)
    steps[...] = parts[:128] + parts[128:256] + parts[256:]
    chain(0)
    weights_first(1)
    lax.fori_loop(2, 4, intra, 0)
    chain(1)
    weights_second(0)
    z_copy.wait()
    enter(0)
    lax.fori_loop(0, 2, finish, 0)
    weights_second(1)
    weights_third(0)
    enter(1)
    lax.fori_loop(2, 4, finish, 0)
    weights_third(1)

    for half in range(2):
        for copy in halo(half):
            copy.wait_send()

    def drain(i):
        send_decay(i).wait_send()
        for s in range(2):
            send_update(s, i).wait_send()
            send_entry(s, i).wait_send()

    each_peer(drain)
    weights_end()


def mix(x_part, bc_part, dt_part, a_log, skip_scale, norm_gain, conv_x, conv_bc, z_part, weight):
    blocks, heads = dt_part.shape[:2]
    cols = x_part.shape[3]
    depth, width = weight.shape
    dma = pltpu.SemaphoreType.DMA
    low, wide = jnp.bfloat16, jnp.float32
    vmem = pl.BlockSpec(memory_space=pltpu.VMEM)
    hbm = pl.BlockSpec(memory_space=pl.ANY)
    return pl.pallas_call(
        mixer_kernel,
        out_shape=(
            jax.ShapeDtypeStruct((blocks, HALF, cols), low),
            jax.ShapeDtypeStruct((4, depth, width // 8), low),
        ),
        in_specs=[vmem] * 8 + [hbm] * 2,
        out_specs=(vmem, hbm),
        scratch_shapes=[
            pltpu.VMEM((2, 2, 16, cols), low),
            pltpu.VMEM((2, 2, 16, 2 * STATE), low),
            pltpu.VMEM((8 + HALF, 256), wide),
            pltpu.VMEM((blocks, HALF, cols), low),
            pltpu.VMEM((blocks, HALF, STATE), low),
            pltpu.VMEM((blocks, HALF, STATE), low),
            pltpu.VMEM((blocks, heads, HALF), wide),
            pltpu.VMEM((blocks, heads, HALF), wide),
            pltpu.VMEM((blocks, HALF, heads), wide),
            pltpu.VMEM((blocks, HALF, 3 * heads), low),
            pltpu.VMEM((blocks, HALF, 3 * heads), low),
            pltpu.VMEM((3 * heads, cols), low),
            pltpu.VMEM((HALF, 256), low),
            pltpu.VMEM((blocks, STATE, cols), low),
            pltpu.VMEM((16, blocks, STATE // 8, cols // 2), low),
            pltpu.VMEM((16, blocks, STATE // 8, cols // 2), low),
            pltpu.VMEM((blocks, STATE, cols), low),
            pltpu.VMEM((8, 128), wide),
            pltpu.VMEM((16, 8, 128), wide),
            pltpu.VMEM((128, cols // 2), wide),
            pltpu.VMEM((blocks, HALF, cols), wide),
            pltpu.VMEM((blocks, HALF, cols), low),
            dma, dma((2, 2)), dma((2, 2)), dma((16,)), dma((16,)), dma((2,)),
            dma((2, 16)), dma((2, 16)), dma((2, 16)), dma((2, 16)),
            dma((4,)), dma((4,)), dma((2, 2)), dma((2, 2)), dma((2, 2)), dma((2, 2)),
            dma((2, 4)), dma((2, 4)),
        ],
        compiler_params=pltpu.CompilerParams(
            collective_id=1, has_side_effects=True, vmem_limit_bytes=56 << 20
        ),
        name="mixer",
    )(x_part, bc_part, dt_part, a_log, skip_scale, norm_gain, conv_x, conv_bc, z_part, weight)


def project_kernel(
    n_ref, w_ref, wr_ref, out_ref,
    act, wts, mid, keep, direct, joined, own, relay, final,
    load_s, act_s, y_s, y_r, mid_s, mid_r, fin_s, fin_r,
):
    z, y_lo, core, x, y_hi = place()
    partner = device(z, y_lo, core, x, 1 - y_hi)
    right = device(z, y_lo, core, (x + 1) % 4, y_hi)
    left = device(z, y_lo, core, (x + 3) % 4, y_hi)
    ways = (right, left)
    tokens, depth = n_ref.shape
    cols = out_ref.shape[1]
    half = cols // 2
    tiles = tokens // HALF

    def rows(t):
        return pl.ds(pl.multiple_of(t * HALF, HALF), HALF)

    def loads(d):
        block = 2 * ((x + REACH[d]) % 4) + y_hi
        src = w_ref.at[:, pl.ds(pl.multiple_of(block * cols, cols), cols)]
        return (
            pltpu.make_async_copy(src, wts.at[d, pl.ds(0, depth)], load_s.at[d, 0]),
            pltpu.make_async_copy(wr_ref.at[d], wts.at[d, pl.ds(depth, depth)], load_s.at[d, 1]),
        )

    own_act = pltpu.make_async_copy(n_ref, act.at[:, pl.ds(0, depth)], act_s)

    def to_partner(t):
        return remote(
            n_ref.at[rows(t)], act.at[rows(t), pl.ds(depth, depth)], y_s.at[t], y_r.at[t], partner
        )

    def pass_on(t, way):
        return remote(
            mid.at[way, rows(t)], relay.at[way, rows(t)], mid_s.at[t, way], mid_r.at[t, way],
            ways[way],
        )

    def send_direct(t, way):
        return remote(
            direct.at[way, rows(t)], final.at[way, 0, rows(t)], fin_s.at[t, way, 0],
            fin_r.at[t, way, 0], ways[way],
        )

    def send_joined(t, way):
        return remote(
            joined.at[way, rows(t)], final.at[way, 1, rows(t)], fin_s.at[t, way, 1],
            fin_r.at[t, way, 1], ways[way],
        )

    own_act.start()
    for d in range(4):
        for copy in loads(d):
            copy.start()
    greet([partner, right, left])
    for t in range(tiles):
        to_partner(t).start()
    own_act.wait()

    def product(t, d, side):
        return jnp.dot(
            act[rows(t)], wts[d, :, side * half : (side + 1) * half],
            preferred_element_type=jnp.float32,
        )

    def ready(t, d):
        @pl.when(t == 0)
        def _():
            for copy in loads(d):
                copy.wait()

    def finish(t):
        for way in range(2):
            send_direct(t, way).wait_recv()
            send_joined(t, way).wait_recv()
        r = rows(t)
        for side in range(2):
            total = own[r, side * half : (side + 1) * half]
            total = total + final[0, 1 - side, r].astype(jnp.float32)
            total = total + final[1, side, r].astype(jnp.float32)
            out_ref[r, side * half : (side + 1) * half] = total.astype(out_ref.dtype)

    def tile(t, carry):
        r = rows(t)
        to_partner(t).wait_recv()
        ready(t, 0)
        for way in range(2):
            mid[way, r] = product(t, 0, way).astype(mid.dtype)
            pass_on(t, way).start()
        for way in range(2):
            ready(t, 1 + way)
            direct[way, r] = product(t, 1 + way, 1 - way).astype(direct.dtype)
            send_direct(t, way).start()
            keep[way, r] = product(t, 1 + way, way)
        ready(t, 3)
        for side in range(2):
            own[r, side * half : (side + 1) * half] = product(t, 3, side)
        for way in range(2):
            pass_on(t, way).wait_recv()
            joined[way, r] = (keep[way, r] + relay[way, r].astype(jnp.float32)).astype(joined.dtype)
            send_joined(t, way).start()

        @pl.when(t > 0)
        def _():
            finish(t - 1)

        return carry

    lax.fori_loop(0, tiles, tile, 0)
    finish(tiles - 1)

    def drain(t, carry):
        to_partner(t).wait_send()
        for way in range(2):
            pass_on(t, way).wait_send()
            send_direct(t, way).wait_send()
            send_joined(t, way).wait_send()
        return carry

    lax.fori_loop(0, tiles, drain, 0)


def project(normed, out_weight, received):
    tokens, depth = normed.shape
    cols = out_weight.shape[1] // 8
    half = cols // 2
    tiles = tokens // HALF
    dma = pltpu.SemaphoreType.DMA
    low, wide = jnp.bfloat16, jnp.float32
    return pl.pallas_call(
        project_kernel,
        out_shape=jax.ShapeDtypeStruct((tokens, cols), low),
        in_specs=[
            pl.BlockSpec(memory_space=pltpu.VMEM),
            pl.BlockSpec(memory_space=pl.ANY),
            pl.BlockSpec(memory_space=pl.ANY),
        ],
        out_specs=pl.BlockSpec(memory_space=pltpu.VMEM),
        scratch_shapes=[
            pltpu.VMEM((tokens, 2 * depth), low),
            pltpu.VMEM((4, 2 * depth, cols), low),
            pltpu.VMEM((2, tokens, half), low),
            pltpu.VMEM((2, tokens, half), wide),
            pltpu.VMEM((2, tokens, half), low),
            pltpu.VMEM((2, tokens, half), low),
            pltpu.VMEM((tokens, cols), wide),
            pltpu.VMEM((2, tokens, half), low),
            pltpu.VMEM((2, 2, tokens, half), low),
            dma((4, 2)), dma, dma((tiles,)), dma((tiles,)), dma((tiles, 2)), dma((tiles, 2)),
            dma((tiles, 2, 2)), dma((tiles, 2, 2)),
        ],
        compiler_params=pltpu.CompilerParams(
            collective_id=2, has_side_effects=True, vmem_limit_bytes=56 << 20
        ),
        name="projection",
    )(normed, out_weight, received)


def mixer(
    x_part, z_part, bc_part, conv_x, conv_bc, dt_part, a_log, skip_scale, norm_gain, out_weight
):
    seq_count, tok_count, cols = x_part.shape
    heads = a_log.shape[0]
    blocks = 2 * seq_count
    by_block = (
        dt_part.reshape(seq_count, heads, 2, HALF).transpose(0, 2, 1, 3).reshape(blocks, heads, HALF)
    )
    normed, received = mix(
        x_part.reshape(seq_count, 2, HALF, cols),
        bc_part.reshape(seq_count, 2, HALF, 2 * STATE),
        by_block,
        a_log.reshape(heads, 1),
        jnp.repeat(skip_scale, HEAD_DIM).reshape(1, cols),
        norm_gain.reshape(1, cols),
        conv_x,
        conv_bc.reshape(KW, 2 * STATE),
        z_part.reshape(blocks, HALF, cols),
        out_weight,
    )
    projected = project(normed.reshape(seq_count * tok_count, cols), out_weight, received)
    return projected.reshape(seq_count, tok_count, projected.shape[1])


def body(x_in, z_in, bc_in, conv_x, conv_bc, dt_raw, a_log, skip_scale, norm_gain, out_weight):
    return mixer(
        x_in, z_in, bc_in, conv_x, conv_bc, dt_raw, a_log, skip_scale, norm_gain, out_weight
    )


def solution(mesh):
    in_specs = (
        P(None, "ctx", "head"),
        P(None, "ctx", "head"),
        P(None, "ctx", None, "head"),
        P(None, "head"),
        P(None, None, "head"),
        P(None, "head", "ctx"),
        P("head"),
        P("head"),
        P("head"),
        P("head", None),
    )
    out_specs = P(None, "ctx", "head")
    return jax.shard_map(body, mesh=mesh, in_specs=in_specs, out_specs=out_specs, check_vma=False)
```

```python
import jax
import jax.numpy as jnp
from jax import lax
from jax.experimental import pallas as pl
from jax.experimental.pallas import tpu as pltpu
from jax.sharding import PartitionSpec as P

HEAD_DIM = 64
STATE = 128
KW = 4
HALF = 192
MESH = pl.DeviceIdType.MESH
REACH = (2, 1, 3, 0)


def place():
    c, h = lax.axis_index("ctx"), lax.axis_index("head")
    return c // 4, (c // 2) % 2, c % 2, h // 2, h % 2


def device(z, y_lo, core, x, y_hi):
    return (z * 4 + y_lo * 2 + core, x * 2 + y_hi)


def remote(src, dst, send_sem, recv_sem, target):
    return pltpu.make_async_remote_copy(
        src_ref=src,
        dst_ref=dst,
        send_sem=send_sem,
        recv_sem=recv_sem,
        device_id=target,
        device_id_type=MESH,
    )


def rounded_parts(values):
    high = values.astype(jnp.bfloat16)
    rest = values - high.astype(jnp.float32)
    middle = rest.astype(jnp.bfloat16)
    low = (rest - middle.astype(jnp.float32)).astype(jnp.bfloat16)
    return jnp.concatenate([high, middle, low], axis=0)


def unit(size):
    rows = lax.broadcasted_iota(jnp.int32, (size, size), 0)
    cols = lax.broadcasted_iota(jnp.int32, (size, size), 1)
    return jnp.where(rows == cols, 1.0, 0.0).astype(jnp.bfloat16)


def by_rows(left, right):
    return lax.dot_general(
        left, right, (((1,), (1,)), ((), ())), preferred_element_type=jnp.float32
    )


def mixer_kernel(
    x_ref, bc_ref, dt_ref, a_ref, skip_ref, gain_ref, taps_ref, taps_bc_ref, z_ref, w_ref,
    out_ref,
    halo_x, halo_bc, wide, xs, bs, cs, cum_row, dt_row, cum_col, tail3, cum3, spread3, skips,
    scaled, upd, sib, comp, got, back, came, give, ent, dec, dec_sib, dec_chip, decs, steps, pace,
    inner, zbuf, act, wts, mid, keep, direct, joined, own, relay, final,
    z_sem, load_s, halo_s, halo_r, dec_s, dec_r, own_s, sib_s, sib_r, upd_s, upd_r, ent_s, ent_r,
    give_s, give_r, in_s, in_r, z_s, z_r, far_s, far_r, core_s, core_r,
    y_s, y_r, mid_s, mid_r, fin_s, fin_r,
):
    f32, bf16 = jnp.float32, jnp.bfloat16
    z, y_lo, core, x, y_hi = place()
    me = lax.axis_index("ctx")
    chip = me // 2
    head = lax.axis_index("head")
    cols = x_ref.shape[3]
    state_rows, lanes = got.shape[2:]
    heads = dt_ref.shape[1]
    depth = wts.shape[1] // 2
    part = depth // 8
    side_cols = cols // 2
    tiles = 4

    partner = device(z, 1 - y_lo, core, x, 1 - y_hi)
    across_y = device(z, y_lo, core, x, 1 - y_hi)
    up = device((z + 1) % 4, y_lo, core, x, y_hi)
    down = device((z + 3) % 4, y_lo, core, x, y_hi)
    other = device(z, y_lo, 1 - core, x, y_hi)
    ways = (
        device(z, y_lo, core, (x + 1) % 4, y_hi),
        device(z, y_lo, core, (x + 3) % 4, y_hi),
    )

    def at(index):
        return (index, head)

    before, after = at((me + 15) % 16), at((me + 1) % 16)

    def fellow(step):
        return (chip + step) % 8

    def of_chip(number):
        return at(2 * number + core)

    def each_fellow(work):
        def step(i, carry):
            work(i)
            return carry

        lax.fori_loop(1, 8, step, 0)

    def load(d):
        block = 2 * ((x + REACH[d]) % 4) + y_hi
        src = w_ref.at[:, pl.ds(pl.multiple_of(block * cols, cols), cols)]
        return pltpu.make_async_copy(src, wts.at[d, pl.ds(0, depth)], load_s.at[d])

    def part_at(step):
        return (((z + step) % 4) * 2 + core) * part

    def held(step):
        return pl.ds(pl.multiple_of(depth + part_at(step), part), part)

    def import_part(d):
        block = 2 * ((x + REACH[d]) % 4) + 1 - y_hi
        src = w_ref.at[
            pl.ds(pl.multiple_of(part_at(0), part), part),
            pl.ds(pl.multiple_of(block * cols, cols), cols),
        ]
        return remote(src, wts.at[d, held(0)], in_s.at[d], in_r.at[d], partner)

    def near(d, way):
        here = wts.at[d, held(0)]
        return remote(here, here, z_s.at[d, way], z_r.at[d, way], down if way else up)

    def far(d, way):
        step = 1 if way else 3
        rows = pl.ds(
            pl.multiple_of(depth + part_at(step) + way * (part // 2), part // 2), part // 2
        )
        here = wts.at[d, rows]
        return remote(here, here, far_s.at[d, way], far_r.at[d, way], down if way else up)

    def across(d, step):
        here = wts.at[d, held(step)]
        return remote(here, here, core_s.at[d, step], core_r.at[d, step], other)

    def weights_first(d):
        import_part(d).wait_recv()
        near(d, 0).start()
        near(d, 1).start()
        across(d, 0).start()

    def weights_second(d):
        for way in range(2):
            near(d, way).wait_recv()
            far(d, way).start()
            across(d, 1 if way else 3).start()

    def weights_third(d):
        far(d, 0).wait_recv()
        far(d, 1).wait_recv()
        across(d, 2).start()

    def weights_ready(d):
        load(d).wait()
        for step in range(4):
            across(d, step).wait_recv()

    def halo(half):
        target = before if half else after
        rows = pl.ds(HALF - 16, 16)
        return (
            remote(
                x_ref.at[:, half, rows], halo_x.at[half], halo_s.at[half, 0], halo_r.at[half, 0],
                target,
            ),
            remote(
                bc_ref.at[:, half, rows], halo_bc.at[half], halo_s.at[half, 1],
                halo_r.at[half, 1], target,
            ),
        )

    def share(number):
        return pl.ds(pl.multiple_of(number * state_rows, state_rows), state_rows)

    def my_lanes(which):
        return pl.ds(pl.multiple_of(which * lanes, lanes), lanes)

    def of_seq(s):
        return pl.ds(2 * s, 2)

    def swap_decay():
        return remote(dec, dec_sib, dec_s.at[0], dec_r.at[0], other)

    def send_decay(step):
        return remote(
            dec_chip, decs.at[chip], dec_s.at[step], dec_r.at[step], of_chip(fellow(step))
        )

    def swap_update(s):
        return remote(
            upd.at[of_seq(s), :, my_lanes(1 - core)], sib.at[of_seq(s)], sib_s.at[s], sib_r.at[s],
            other,
        )

    def send_update(s, step):
        owner = fellow(step)
        return remote(
            comp.at[of_seq(s), share(owner)], got.at[chip, of_seq(s)], upd_s.at[s, step],
            upd_r.at[s, step], of_chip(owner),
        )

    def send_entry(s, step):
        target = fellow(step)
        return remote(
            back.at[target, of_seq(s)], came.at[of_seq(s), share(chip)], ent_s.at[s, step],
            ent_r.at[s, step], of_chip(target),
        )

    def give_entry(s):
        return remote(
            give.at[of_seq(s)], ent.at[of_seq(s), :, my_lanes(core)], give_s.at[s], give_r.at[s],
            other,
        )

    def keep_update(s):
        return pltpu.make_async_copy(
            comp.at[of_seq(s), share(chip)], got.at[chip, of_seq(s)], own_s.at[s, 0]
        )

    def keep_entry(s):
        return pltpu.make_async_copy(
            back.at[chip, of_seq(s)], came.at[of_seq(s), share(chip)], own_s.at[s, 1]
        )

    z_copy = pltpu.make_async_copy(z_ref, zbuf, z_sem)
    z_copy.start()
    barrier = pltpu.get_barrier_semaphore()

    def hello(target):
        pl.semaphore_signal(barrier, inc=1, device_id=target, device_id_type=MESH)

    each_fellow(lambda i: hello(of_chip(fellow(i))))
    hello(at((me + 15 + 2 * core) % 16))
    for target in (other, partner, across_y) + ways:
        hello(target)

    row_id = lax.broadcasted_iota(jnp.int32, (HALF, HALF), 0)
    col_id = lax.broadcasted_iota(jnp.int32, (HALF, HALF), 1)
    causal = row_id >= col_id
    eye = unit(HALF)

    def three(values, count):
        return values[:count] + values[count : 2 * count] + values[2 * count :]

    def three_cols(values, count):
        return values[:, :count] + values[:, count : 2 * count] + values[:, 2 * count :]

    rate = -jnp.exp(three_cols(by_rows(unit(heads), rounded_parts(a_ref[...])), 1))
    dec[...] = jnp.zeros_like(dec)
    source = lax.broadcasted_iota(jnp.int32, (2 * HALF, HALF), 0)
    goal = lax.broadcasted_iota(jnp.int32, (2 * HALF, HALF), 1)
    for s in range(2):
        raw = dt_ref[s]
        both = jnp.maximum(raw, 0.0) + jnp.log1p(jnp.exp(-jnp.abs(raw)))
        sizes = rounded_parts(both)
        falls = rounded_parts(both * rate)
        for half in range(2):
            b = 2 * s + half
            low = HALF * half
            pick = jnp.where(source == goal + low, 1.0, 0.0).astype(bf16)
            ahead = jnp.where((source >= low) & (source <= goal + low), 1.0, 0.0).astype(bf16)
            step_size = three(jnp.dot(sizes, pick, preferred_element_type=f32), heads)
            cum = three(jnp.dot(falls, ahead, preferred_element_type=f32), heads)
            dt_row[b] = step_size
            cum_row[b] = cum
            col = three_cols(by_rows(eye, rounded_parts(cum)), heads)
            cum_col[b] = col
            dec[b : b + 1, :heads] = jnp.exp(col[HALF - 1 :])
            tail = jnp.exp(cum[:, HALF - 1 :] - cum) * step_size
            tail3[b] = by_rows(eye, rounded_parts(tail)).astype(bf16)
            cum3[b] = by_rows(eye, rounded_parts(jnp.exp(cum))).astype(bf16)
    of_head = lax.broadcasted_iota(jnp.int32, spread3.shape, 1) // HEAD_DIM
    of_part = lax.broadcasted_iota(jnp.int32, spread3.shape, 0) % heads
    spread3[...] = jnp.where(of_head == of_part, 1.0, 0.0).astype(bf16)
    skips[...] = three(
        jnp.dot(rounded_parts(skip_ref[...]), spread3[:heads], preferred_element_type=f32), 1
    )

    pl.semaphore_wait(barrier, 13)
    for half in range(2):
        for copy in halo(half):
            copy.start()
    swap_decay().start()
    for d in range(4):
        import_part(d).start()
    for d in range(4):
        load(d).start()

    head_id = lax.broadcasted_iota(jnp.int32, (128, lanes), 0)
    lane_head = lax.broadcasted_iota(jnp.int32, (128, lanes), 1) // HEAD_DIM
    picks = jnp.where(head_id == lane_head + core * (lanes // HEAD_DIM), 1.0, 0.0).astype(bf16)

    def to_lanes(values):
        count = values.shape[0]
        return three(jnp.dot(rounded_parts(values), picks, preferred_element_type=f32), count)

    swap_decay().wait_recv()
    dec_chip[...] = dec[...] * dec_sib[...]
    each_fellow(lambda i: send_decay(i).start())
    decs[chip] = dec_chip[...]
    pace[0] = to_lanes(dec[...])
    pace[1] = to_lanes(dec_sib[...])
    for half in range(2):
        for copy in halo(half):
            copy.wait_recv()

    turn = unit(STATE)
    chunk = 256
    band = 64

    def convolve(s, half, start, width, src, lead_ref, tap, put):
        earlier = lead_ref[0, s, :, pl.ds(start, width)]
        earlier = jnp.where(me == 0, jnp.zeros_like(earlier), earlier)
        turned = jnp.where(
            me == 15, src[s, 0, HALF - 16 :, pl.ds(start, width)],
            lead_ref[1, s, :, pl.ds(start, width)],
        )
        lead = jnp.where(half == 0, earlier, turned)
        wide[0:8] = lead.astype(f32)[8:]
        wide[8:] = src[s, half, :, pl.ds(start, width)].astype(f32)
        for r in range(0, HALF, band):
            total = tap[0:1] * wide[r + 5 : r + 5 + band]
            for k in range(1, KW):
                total = total + tap[k : k + 1] * wide[r + 5 + k : r + 5 + k + band]
            put(r, (total / (1.0 + jnp.exp(-total))).astype(bf16))

    def front(b, carry):
        s, half = b // 2, b % 2

        def put_bc(r, values):
            bs[b, r : r + band] = values[:, :STATE]
            cs[b, r : r + band] = values[:, STATE:]

        taps_bc = jnp.concatenate([taps_bc_ref[:, 0], taps_bc_ref[:, 1]], axis=1)
        convolve(s, half, 0, chunk, bc_ref, halo_bc, taps_bc, put_bc)
        bs_turned = by_rows(turn, bs[b]).astype(bf16)

        def columns(i, carry):
            start = pl.multiple_of(i * chunk, chunk)

            def put(r, values):
                xs[b, r : r + band, pl.ds(start, chunk)] = values

            convolve(s, half, start, chunk, x_ref, halo_x, taps_ref[:, pl.ds(start, chunk)], put)
            for r in range(0, HALF, band):
                factor = jnp.dot(
                    tail3[b, r : r + band], spread3[:, pl.ds(start, chunk)],
                    preferred_element_type=f32,
                )
                scaled[r : r + band] = (
                    factor * xs[b, r : r + band, pl.ds(start, chunk)].astype(f32)
                ).astype(bf16)
            upd[b, :, pl.ds(start, chunk)] = jnp.dot(
                bs_turned, scaled[...], preferred_element_type=f32
            ).astype(bf16)
            return carry

        lax.fori_loop(0, cols // chunk, columns, 0)
        return carry

    def join(s):
        swap_update(s).wait_recv()
        for half in range(2):
            b = 2 * s + half
            mine = upd[b, :, my_lanes(core)].astype(f32)
            theirs = sib[b].astype(f32)
            am_first = core == half
            later = jnp.where(am_first, pace[1, b : b + 1], pace[0, b : b + 1])
            comp[b] = (
                later * jnp.where(am_first, mine, theirs) + jnp.where(am_first, theirs, mine)
            ).astype(bf16)
        each_fellow(lambda i: send_update(s, i).start())
        keep_update(s).start()

    first = 128

    def intra(b, carry):
        scores = jnp.where(causal, by_rows(cs[b], bs[b]), 0.0)
        low_half = lax.broadcasted_iota(jnp.int32, (1, 128), 1) < HEAD_DIM
        for p in range(heads // 2):
            tops, ends = [], []
            for h in (2 * p, 2 * p + 1):
                col = cum_col[b, :, h : h + 1]
                row = cum_row[b, h : h + 1]
                size = dt_row[b, h : h + 1]
                gap = jnp.minimum(col[:first] - row[:, :first], 0.0)
                tops.append(
                    (scores[:first, :first] * jnp.exp(gap) * size[:, :first]).astype(bf16)
                )
                gap = jnp.minimum(col[first:] - row, 0.0)
                ends.append((scores[first:] * jnp.exp(gap) * size).astype(bf16))
            pair = slice(128 * p, 128 * p + 128)
            top = jnp.dot(
                jnp.concatenate(tops, axis=0), xs[b, :first, pair], preferred_element_type=f32
            )
            end = jnp.dot(
                jnp.concatenate(ends, axis=0), xs[b, :, pair], preferred_element_type=f32
            )
            inner[b, :first, pair] = jnp.where(low_half, top[:first], top[first:])
            rest = HALF - first
            inner[b, first:, pair] = jnp.where(low_half, end[:rest], end[rest:])
        return carry

    def chain(s):
        each_fellow(lambda i: send_update(s, i).wait_recv())
        keep_update(s).wait()
        state = jnp.zeros((state_rows, lanes), f32)
        for i in range(16):
            c, half = (i, 0) if i < 8 else (15 - i, 1)
            b = 2 * s + half
            back[c, b] = state.astype(bf16)
            state = steps[8 * c + b : 8 * c + b + 1] * state + got[c, b].astype(f32)
        each_fellow(lambda i: send_entry(s, i).start())
        keep_entry(s).start()

    def enter(s):
        each_fellow(lambda i: send_entry(s, i).wait_recv())
        keep_entry(s).wait()
        for half in range(2):
            b = 2 * s + half
            mine = upd[b, :, my_lanes(core)].astype(f32)
            theirs = sib[b].astype(f32)
            am_first = core == half
            entry = came[b].astype(f32)
            rate_first = jnp.where(am_first, pace[0, b : b + 1], pace[1, b : b + 1])
            second = rate_first * entry + jnp.where(am_first, mine, theirs)
            ent[b, :, my_lanes(core)] = jnp.where(am_first, entry, second).astype(bf16)
            give[b] = jnp.where(am_first, second, entry).astype(bf16)
        give_entry(s).start()

    def tile_rows(t):
        return pl.ds(pl.multiple_of(t * HALF, HALF), HALF)

    def to_partner(t):
        return remote(
            act.at[tile_rows(t), pl.ds(0, depth)], act.at[tile_rows(t), pl.ds(depth, depth)],
            y_s.at[t], y_r.at[t], across_y,
        )

    def finish(b, carry):
        squares = [jnp.zeros((96, 128), f32)] * 2
        for q in range(cols // chunk):
            part_cols = slice(q * chunk, (q + 1) * chunk)
            for i in range(2):
                r = slice(96 * i, 96 * i + 96)
                carried = jnp.dot(cs[b, r], ent[b, :, part_cols], preferred_element_type=f32)
                factor = jnp.dot(cum3[b, r], spread3[:, part_cols], preferred_element_type=f32)
                total = inner[b, r, part_cols] + factor * carried
                total = total + skips[:, part_cols] * xs[b, r, part_cols].astype(f32)
                gate = zbuf[b, r, part_cols].astype(f32)
                total = total * (gate / (1.0 + jnp.exp(-gate)))
                inner[b, r, part_cols] = total
                square = total * total
                squares[i] = squares[i] + square[:, :128] + square[:, 128:]
        for i in range(2):
            spread = jnp.sum(squares[i], axis=1, keepdims=True) * (1.0 / cols)
            scale = lax.rsqrt(spread + 1e-05)
            r = slice(96 * i, 96 * i + 96)
            to = pl.ds(pl.multiple_of(b * HALF + 96 * i, 96), 96)
            for q in range(cols // chunk):
                part_cols = slice(q * chunk, (q + 1) * chunk)
                act[to, part_cols] = (
                    inner[b, r, part_cols] * scale * gain_ref[:, part_cols]
                ).astype(bf16)
        to_partner(b).start()
        return carry

    def pass_on(t, way):
        return remote(
            mid.at[way, tile_rows(t)], relay.at[way, tile_rows(t)], mid_s.at[t, way],
            mid_r.at[t, way], ways[way],
        )

    def send_direct(t, way):
        return remote(
            direct.at[way, tile_rows(t)], final.at[way, 0, tile_rows(t)], fin_s.at[t, way, 0],
            fin_r.at[t, way, 0], ways[way],
        )

    def send_joined(t, way):
        return remote(
            joined.at[way, tile_rows(t)], final.at[way, 1, tile_rows(t)], fin_s.at[t, way, 1],
            fin_r.at[t, way, 1], ways[way],
        )

    def side_of(side):
        return slice(side * side_cols, (side + 1) * side_cols)

    def product(t, d, side):
        return jnp.dot(
            act[tile_rows(t)], wts[d, :, side_of(side)], preferred_element_type=f32
        )

    def project_far(t):
        to_partner(t).wait_recv()
        for way in range(2):
            mid[way, tile_rows(t)] = product(t, 0, way).astype(bf16)
            pass_on(t, way).start()

    def project_near(t, way):
        direct[way, tile_rows(t)] = product(t, 1 + way, 1 - way).astype(bf16)
        send_direct(t, way).start()
        keep[way, tile_rows(t)] = product(t, 1 + way, way)

    def project_join(t):
        for way in range(2):
            pass_on(t, way).wait_recv()
            r = tile_rows(t)
            joined[way, r] = (keep[way, r] + relay[way, r].astype(f32)).astype(bf16)
            send_joined(t, way).start()

    def project_own(t):
        for side in range(2):
            own[tile_rows(t), side_of(side)] = product(t, 3, side)

    def project_end(t):
        r = tile_rows(t)
        for way in range(2):
            send_direct(t, way).wait_recv()
            send_joined(t, way).wait_recv()
        for side in range(2):
            total = own[r, side_of(side)] + final[0, 1 - side, r].astype(f32)
            total = total + final[1, side, r].astype(f32)
            out_ref[r, side_of(side)] = total.astype(bf16)

    for s in range(2):
        lax.fori_loop(2 * s, 2 * s + 2, front, 0)
        swap_update(s).start()
    weights_first(0)
    join(0)
    join(1)
    weights_first(1)
    lax.fori_loop(0, 2, intra, 0)
    each_fellow(lambda i: send_decay(i).wait_recv())
    steps[...] = to_lanes(decs[...].reshape(64, 128))
    chain(0)
    weights_second(0)
    weights_first(2)
    lax.fori_loop(2, 4, intra, 0)
    chain(1)
    weights_second(1)
    weights_first(3)
    weights_third(0)
    z_copy.wait()
    enter(0)
    give_entry(0).wait_recv()
    lax.fori_loop(0, 2, finish, 0)
    enter(1)
    weights_second(2)
    weights_third(1)
    give_entry(1).wait_recv()
    lax.fori_loop(2, 4, finish, 0)
    weights_second(3)
    weights_third(2)
    weights_ready(0)
    project_far(0)
    weights_third(3)
    weights_ready(1)
    project_near(0, 0)
    weights_ready(2)
    project_near(0, 1)

    def middle(t, carry):
        project_far(t)
        for way in range(2):
            project_near(t, way)
        project_join(t - 1)
        return carry

    lax.fori_loop(1, tiles, middle, 0)
    project_join(tiles - 1)
    weights_ready(3)

    def last(t, carry):
        project_own(t)
        project_end(t)
        return carry

    lax.fori_loop(0, tiles, last, 0)

    for half in range(2):
        for copy in halo(half):
            copy.wait_send()
    swap_decay().wait_send()
    for s in range(2):
        swap_update(s).wait_send()
        give_entry(s).wait_send()

    def drain(i):
        send_decay(i).wait_send()
        for s in range(2):
            send_update(s, i).wait_send()
            send_entry(s, i).wait_send()

    each_fellow(drain)
    for d in range(4):
        import_part(d).wait_send()
        for way in range(2):
            near(d, way).wait_send()
            far(d, way).wait_send()
        for step in range(4):
            across(d, step).wait_send()

    def drain_tile(t, carry):
        to_partner(t).wait_send()
        for way in range(2):
            pass_on(t, way).wait_send()
            send_direct(t, way).wait_send()
            send_joined(t, way).wait_send()
        return carry

    lax.fori_loop(0, tiles, drain_tile, 0)


def mix(x_part, bc_part, dt_part, a_log, skip_scale, norm_gain, conv_x, conv_bc, z_part, weight):
    blocks = 4
    heads = dt_part.shape[1]
    cols = x_part.shape[3]
    depth = weight.shape[0]
    tokens = blocks * HALF
    half = cols // 2
    dma = pltpu.SemaphoreType.DMA
    low, wide = jnp.bfloat16, jnp.float32
    vmem = pl.BlockSpec(memory_space=pltpu.VMEM)
    hbm = pl.BlockSpec(memory_space=pl.ANY)
    return pl.pallas_call(
        mixer_kernel,
        out_shape=jax.ShapeDtypeStruct((tokens, cols), low),
        in_specs=[vmem] * 8 + [hbm] * 2,
        out_specs=vmem,
        scratch_shapes=[
            pltpu.VMEM((2, 2, 16, cols), low),
            pltpu.VMEM((2, 2, 16, 2 * STATE), low),
            pltpu.VMEM((8 + HALF, 256), wide),
            pltpu.VMEM((blocks, HALF, cols), low),
            pltpu.VMEM((blocks, HALF, STATE), low),
            pltpu.VMEM((blocks, HALF, STATE), low),
            pltpu.VMEM((blocks, heads, HALF), wide),
            pltpu.VMEM((blocks, heads, HALF), wide),
            pltpu.VMEM((blocks, HALF, heads), wide),
            pltpu.VMEM((blocks, HALF, 3 * heads), low),
            pltpu.VMEM((blocks, HALF, 3 * heads), low),
            pltpu.VMEM((3 * heads, cols), low),
            pltpu.VMEM((1, cols), wide),
            pltpu.VMEM((HALF, 256), low),
            pltpu.VMEM((blocks, STATE, cols), low),
            pltpu.VMEM((blocks, STATE, half), low),
            pltpu.VMEM((blocks, STATE, half), low),
            pltpu.VMEM((8, blocks, STATE // 8, half), low),
            pltpu.VMEM((8, blocks, STATE // 8, half), low),
            pltpu.VMEM((blocks, STATE, half), low),
            pltpu.VMEM((blocks, STATE, half), low),
            pltpu.VMEM((blocks, STATE, cols), low),
            pltpu.VMEM((8, 128), wide),
            pltpu.VMEM((8, 128), wide),
            pltpu.VMEM((8, 128), wide),
            pltpu.VMEM((8, 8, 128), wide),
            pltpu.VMEM((64, half), wide),
            pltpu.VMEM((2, 8, half), wide),
            pltpu.VMEM((blocks, HALF, cols), wide),
            pltpu.VMEM((blocks, HALF, cols), low),
            pltpu.VMEM((tokens, 2 * depth), low),
            pltpu.VMEM((4, 2 * depth, cols), low),
            pltpu.VMEM((2, tokens, half), low),
            pltpu.VMEM((2, tokens, half), wide),
            pltpu.VMEM((2, tokens, half), low),
            pltpu.VMEM((2, tokens, half), low),
            pltpu.VMEM((tokens, cols), wide),
            pltpu.VMEM((2, tokens, half), low),
            pltpu.VMEM((2, 2, tokens, half), low),
            dma, dma((4,)), dma((2, 2)), dma((2, 2)), dma((8,)), dma((8,)), dma((2, 2)),
            dma((2,)), dma((2,)), dma((2, 8)), dma((2, 8)), dma((2, 8)), dma((2, 8)),
            dma((2,)), dma((2,)), dma((4,)), dma((4,)), dma((4, 2)), dma((4, 2)),
            dma((4, 2)), dma((4, 2)), dma((4, 4)), dma((4, 4)),
            dma((blocks,)), dma((blocks,)), dma((blocks, 2)), dma((blocks, 2)),
            dma((blocks, 2, 2)), dma((blocks, 2, 2)),
        ],
        compiler_params=pltpu.CompilerParams(
            collective_id=1, has_side_effects=True, vmem_limit_bytes=60 << 20
        ),
        name="mixer",
    )(x_part, bc_part, dt_part, a_log, skip_scale, norm_gain, conv_x, conv_bc, z_part, weight)


def mixer(
    x_part, z_part, bc_part, conv_x, conv_bc, dt_part, a_log, skip_scale, norm_gain, out_weight
):
    seq_count, tok_count, cols = x_part.shape
    heads = a_log.shape[0]
    projected = mix(
        x_part.reshape(seq_count, 2, HALF, cols),
        bc_part.reshape(seq_count, 2, HALF, 2 * STATE),
        dt_part,
        a_log.reshape(1, heads),
        skip_scale.reshape(1, heads),
        norm_gain.reshape(1, cols),
        conv_x,
        conv_bc,
        z_part.reshape(2 * seq_count, HALF, cols),
        out_weight,
    )
    return projected.reshape(seq_count, tok_count, cols)


def body(x_in, z_in, bc_in, conv_x, conv_bc, dt_raw, a_log, skip_scale, norm_gain, out_weight):
    return mixer(
        x_in, z_in, bc_in, conv_x, conv_bc, dt_raw, a_log, skip_scale, norm_gain, out_weight
    )


def solution(mesh):
    in_specs = (
        P(None, "ctx", "head"),
        P(None, "ctx", "head"),
        P(None, "ctx", None, "head"),
        P(None, "head"),
        P(None, None, "head"),
        P(None, "head", "ctx"),
        P("head"),
        P("head"),
        P("head"),
        P("head", None),
    )
    out_specs = P(None, "ctx", "head")
    return jax.shard_map(body, mesh=mesh, in_specs=in_specs, out_specs=out_specs, check_vma=False)
```

```python
import jax
import jax.numpy as jnp
from jax import lax
from jax.experimental import pallas as pl
from jax.experimental.pallas import tpu as pltpu
from jax.sharding import PartitionSpec as P

HEAD_DIM = 64
STATE = 128
KW = 4
HALF = 192
MESH = pl.DeviceIdType.MESH
REACH = (2, 1, 3, 0)


def place():
    c, h = lax.axis_index("ctx"), lax.axis_index("head")
    return c // 4, (c // 2) % 2, c % 2, h // 2, h % 2


def device(z, y_lo, core, x, y_hi):
    return (z * 4 + y_lo * 2 + core, x * 2 + y_hi)


def remote(src, dst, send_sem, recv_sem, target):
    return pltpu.make_async_remote_copy(
        src_ref=src,
        dst_ref=dst,
        send_sem=send_sem,
        recv_sem=recv_sem,
        device_id=target,
        device_id_type=MESH,
    )


def rounded_parts(values):
    high = values.astype(jnp.bfloat16)
    rest = values - high.astype(jnp.float32)
    middle = rest.astype(jnp.bfloat16)
    low = (rest - middle.astype(jnp.float32)).astype(jnp.bfloat16)
    return jnp.concatenate([high, middle, low], axis=0)


def unit(size):
    rows = lax.broadcasted_iota(jnp.int32, (size, size), 0)
    cols = lax.broadcasted_iota(jnp.int32, (size, size), 1)
    return jnp.where(rows == cols, 1.0, 0.0).astype(jnp.bfloat16)


def by_rows(left, right):
    return lax.dot_general(
        left, right, (((1,), (1,)), ((), ())), preferred_element_type=jnp.float32
    )


def mixer_kernel(
    x_ref, bc_ref, dt_ref, a_ref, skip_ref, gain_ref, taps_ref, taps_bc_ref, z_ref, w_ref,
    out_ref,
    halo_x, halo_bc, wide, xs, bs, cs, cum_row, dt_row, cum_col, tail3, cum3, spread3, skips,
    scaled, upd, sib, comp, got, back, came, give, ent, dec, dec_sib, dec_chip, decs, steps, pace,
    inner, zbuf, act, wts, mid, keep, direct, joined, own, relay, final,
    z_sem, load_s, halo_s, halo_r, dec_s, dec_r, own_s, sib_s, sib_r, upd_s, upd_r, ent_s, ent_r,
    give_s, give_r, in_s, in_r, side_s, side_r, near_s, near_r, far_s, far_r, core_s, core_r,
    y_s, y_r, mid_s, mid_r, fin_s, fin_r,
):
    f32, bf16 = jnp.float32, jnp.bfloat16
    z, y_lo, core, x, y_hi = place()
    me = lax.axis_index("ctx")
    chip = me // 2
    head = lax.axis_index("head")
    cols = x_ref.shape[3]
    state_rows, lanes = got.shape[2:]
    heads = dt_ref.shape[1]
    depth = wts.shape[1] // 2
    part = depth // 16
    side_cols = cols // 2
    tiles = 4

    partner = device(z, 1 - y_lo, core, x, 1 - y_hi)
    across_y = device(z, y_lo, core, x, 1 - y_hi)
    up = device((z + 1) % 4, y_lo, core, x, y_hi)
    down = device((z + 3) % 4, y_lo, core, x, y_hi)
    beside = device(z, 1 - y_lo, core, x, y_hi)
    other = device(z, y_lo, 1 - core, x, y_hi)
    ways = (
        device(z, y_lo, core, (x + 1) % 4, y_hi),
        device(z, y_lo, core, (x + 3) % 4, y_hi),
    )

    def at(index):
        return (index, head)

    before, after = at((me + 15) % 16), at((me + 1) % 16)

    def fellow(step):
        return (chip + step) % 8

    def of_chip(number):
        return at(2 * number + core)

    def each_fellow(work):
        def step(i, carry):
            work(i)
            return carry

        lax.fori_loop(1, 8, step, 0)

    def load(d):
        block = 2 * ((x + REACH[d]) % 4) + y_hi
        src = w_ref.at[:, pl.ds(pl.multiple_of(block * cols, cols), cols)]
        return pltpu.make_async_copy(src, wts.at[d, pl.ds(0, depth)], load_s.at[d])

    def piece(step, low, base, count=1):
        number = (((z + step) % 4) * 2 + core) * 2 + low
        return pl.ds(pl.multiple_of(base + number * part, part), count * part)

    def import_part(d):
        block = 2 * ((x + REACH[d]) % 4) + 1 - y_hi
        rows = piece(0, 1 - y_lo, 0)
        src = w_ref.at[rows, pl.ds(pl.multiple_of(block * cols, cols), cols)]
        there = wts.at[d, piece(0, 1 - y_lo, depth)]
        return remote(src, there, in_s.at[d], in_r.at[d], partner)

    def swap_part(d):
        here = wts.at[d, piece(0, y_lo, depth)]
        return remote(here, here, side_s.at[d], side_r.at[d], beside)

    def near(d, way, swapped):
        here = wts.at[d, piece(0, 1 - y_lo if swapped else y_lo, depth)]
        return remote(
            here, here, near_s.at[d, way, swapped], near_r.at[d, way, swapped],
            down if way else up,
        )

    def far(d, way):
        here = wts.at[d, piece(1 if way else 3, way, depth)]
        return remote(here, here, far_s.at[d, way], far_r.at[d, way], down if way else up)

    def across(d, number):
        if number < 2:
            rows = piece(0, 1 - y_lo if number else y_lo, depth)
        else:
            rows = piece((1, 3, 2)[number - 2], 0, depth, 2)
        here = wts.at[d, rows]
        return remote(here, here, core_s.at[d, number], core_r.at[d, number], other)

    def weights_in(d):
        import_part(d).wait_recv()
        swap_part(d).start()
        across(d, 0).start()

    def weights_near(d, swapped):
        if swapped:
            swap_part(d).wait_recv()
            across(d, 1).start()
        for way in range(2):
            near(d, way, swapped).start()

    def weights_far(d):
        for way in range(2):
            for swapped in range(2):
                near(d, way, swapped).wait_recv()
            far(d, way).start()
            across(d, 2 if way else 3).start()

    def weights_last(d):
        far(d, 0).wait_recv()
        far(d, 1).wait_recv()
        across(d, 4).start()

    def weights_ready(d):
        load(d).wait()
        for number in range(5):
            across(d, number).wait_recv()

    def halo(half):
        target = before if half else after
        rows = pl.ds(HALF - 16, 16)
        return (
            remote(
                x_ref.at[:, half, rows], halo_x.at[half], halo_s.at[half, 0], halo_r.at[half, 0],
                target,
            ),
            remote(
                bc_ref.at[:, half, rows], halo_bc.at[half], halo_s.at[half, 1],
                halo_r.at[half, 1], target,
            ),
        )

    def share(number):
        return pl.ds(pl.multiple_of(number * state_rows, state_rows), state_rows)

    def my_lanes(which):
        return pl.ds(pl.multiple_of(which * lanes, lanes), lanes)

    def of_seq(s):
        return pl.ds(2 * s, 2)

    def swap_decay():
        return remote(dec, dec_sib, dec_s.at[0], dec_r.at[0], other)

    def send_decay(step):
        return remote(
            dec_chip, decs.at[chip], dec_s.at[step], dec_r.at[step], of_chip(fellow(step))
        )

    def swap_update(s):
        return remote(
            upd.at[of_seq(s), :, my_lanes(1 - core)], sib.at[of_seq(s)], sib_s.at[s], sib_r.at[s],
            other,
        )

    def send_update(s, step):
        owner = fellow(step)
        return remote(
            comp.at[of_seq(s), share(owner)], got.at[chip, of_seq(s)], upd_s.at[s, step],
            upd_r.at[s, step], of_chip(owner),
        )

    def send_entry(s, step):
        target = fellow(step)
        return remote(
            back.at[target, of_seq(s)], came.at[of_seq(s), share(chip)], ent_s.at[s, step],
            ent_r.at[s, step], of_chip(target),
        )

    def give_entry(s):
        return remote(
            give.at[of_seq(s)], ent.at[of_seq(s), :, my_lanes(core)], give_s.at[s], give_r.at[s],
            other,
        )

    def keep_update(s):
        return pltpu.make_async_copy(
            comp.at[of_seq(s), share(chip)], got.at[chip, of_seq(s)], own_s.at[s, 0]
        )

    def keep_entry(s):
        return pltpu.make_async_copy(
            back.at[chip, of_seq(s)], came.at[of_seq(s), share(chip)], own_s.at[s, 1]
        )

    z_copy = pltpu.make_async_copy(z_ref, zbuf, z_sem)
    z_copy.start()
    barrier = pltpu.get_barrier_semaphore()

    def hello(target):
        pl.semaphore_signal(barrier, inc=1, device_id=target, device_id_type=MESH)

    each_fellow(lambda i: hello(of_chip(fellow(i))))
    hello(at((me + 15 + 2 * core) % 16))
    for target in (other, partner, across_y) + ways:
        hello(target)

    row_id = lax.broadcasted_iota(jnp.int32, (HALF, HALF), 0)
    col_id = lax.broadcasted_iota(jnp.int32, (HALF, HALF), 1)
    causal = row_id >= col_id
    eye = unit(HALF)

    def three(values, count):
        return values[:count] + values[count : 2 * count] + values[2 * count :]

    def three_cols(values, count):
        return values[:, :count] + values[:, count : 2 * count] + values[:, 2 * count :]

    rate = -jnp.exp(three_cols(by_rows(unit(heads), rounded_parts(a_ref[...])), 1))
    dec[...] = jnp.zeros_like(dec)
    source = lax.broadcasted_iota(jnp.int32, (2 * HALF, HALF), 0)
    goal = lax.broadcasted_iota(jnp.int32, (2 * HALF, HALF), 1)
    def decays(s):
        raw = dt_ref[s]
        both = jnp.maximum(raw, 0.0) + jnp.log1p(jnp.exp(-jnp.abs(raw)))
        sizes = rounded_parts(both)
        falls = rounded_parts(both * rate)
        for half in range(2):
            b = 2 * s + half
            low = HALF * half
            pick = jnp.where(source == goal + low, 1.0, 0.0).astype(bf16)
            ahead = jnp.where((source >= low) & (source <= goal + low), 1.0, 0.0).astype(bf16)
            step_size = three(jnp.dot(sizes, pick, preferred_element_type=f32), heads)
            cum = three(jnp.dot(falls, ahead, preferred_element_type=f32), heads)
            dt_row[b] = step_size
            cum_row[b] = cum
            col = three_cols(by_rows(eye, rounded_parts(cum)), heads)
            cum_col[b] = col
            dec[b : b + 1, :heads] = jnp.exp(col[HALF - 1 :])
            tail = jnp.exp(cum[:, HALF - 1 :] - cum) * step_size
            tail3[b] = by_rows(eye, rounded_parts(tail)).astype(bf16)
            cum3[b] = by_rows(eye, rounded_parts(jnp.exp(cum))).astype(bf16)
    decays(0)
    pl.semaphore_wait(barrier, 13)
    for half in range(2):
        for copy in halo(half):
            copy.start()
    for d in range(4):
        import_part(d).start()
    decays(1)
    swap_decay().start()
    for d in range(4):
        load(d).start()
    of_head = lax.broadcasted_iota(jnp.int32, spread3.shape, 1) // HEAD_DIM
    of_part = lax.broadcasted_iota(jnp.int32, spread3.shape, 0) % heads
    spread3[...] = jnp.where(of_head == of_part, 1.0, 0.0).astype(bf16)
    skips[...] = three(
        jnp.dot(rounded_parts(skip_ref[...]), spread3[:heads], preferred_element_type=f32), 1
    )

    head_id = lax.broadcasted_iota(jnp.int32, (128, lanes), 0)
    lane_head = lax.broadcasted_iota(jnp.int32, (128, lanes), 1) // HEAD_DIM
    picks = jnp.where(head_id == lane_head + core * (lanes // HEAD_DIM), 1.0, 0.0).astype(bf16)

    def to_lanes(values):
        count = values.shape[0]
        return three(jnp.dot(rounded_parts(values), picks, preferred_element_type=f32), count)

    def chip_decays():
        swap_decay().wait_recv()
        dec_chip[...] = dec[...] * dec_sib[...]
        each_fellow(lambda i: send_decay(i).start())
        decs[chip] = dec_chip[...]
        pace[0] = to_lanes(dec[...])
        pace[1] = to_lanes(dec_sib[...])

    turn = unit(STATE)
    chunk = 256
    band = 64

    def convolve(s, half, start, width, src, lead_ref, tap, put):
        earlier = lead_ref[0, s, :, pl.ds(start, width)]
        earlier = jnp.where(me == 0, jnp.zeros_like(earlier), earlier)
        turned = jnp.where(
            me == 15, src[s, 0, HALF - 16 :, pl.ds(start, width)],
            lead_ref[1, s, :, pl.ds(start, width)],
        )
        lead = jnp.where(half == 0, earlier, turned)
        wide[0:8] = lead.astype(f32)[8:]
        wide[8:] = src[s, half, :, pl.ds(start, width)].astype(f32)
        for r in range(0, HALF, band):
            total = tap[0:1] * wide[r + 5 : r + 5 + band]
            for k in range(1, KW):
                total = total + tap[k : k + 1] * wide[r + 5 + k : r + 5 + k + band]
            put(r, (total / (1.0 + jnp.exp(-total))).astype(bf16))

    def front(b, carry):
        s, half = b // 2, b % 2

        def put_bc(r, values):
            bs[b, r : r + band] = values[:, :STATE]
            cs[b, r : r + band] = values[:, STATE:]

        taps_bc = jnp.concatenate([taps_bc_ref[:, 0], taps_bc_ref[:, 1]], axis=1)
        convolve(s, half, 0, chunk, bc_ref, halo_bc, taps_bc, put_bc)
        bs_turned = by_rows(turn, bs[b]).astype(bf16)

        def columns(i, carry):
            start = pl.multiple_of(i * chunk, chunk)

            def put(r, values):
                xs[b, r : r + band, pl.ds(start, chunk)] = values

            convolve(s, half, start, chunk, x_ref, halo_x, taps_ref[:, pl.ds(start, chunk)], put)
            for r in range(0, HALF, band):
                factor = jnp.dot(
                    tail3[b, r : r + band], spread3[:, pl.ds(start, chunk)],
                    preferred_element_type=f32,
                )
                scaled[r : r + band] = (
                    factor * xs[b, r : r + band, pl.ds(start, chunk)].astype(f32)
                ).astype(bf16)
            upd[b, :, pl.ds(start, chunk)] = jnp.dot(
                bs_turned, scaled[...], preferred_element_type=f32
            ).astype(bf16)
            return carry

        lax.fori_loop(0, cols // chunk, columns, 0)
        return carry

    def join(s):
        swap_update(s).wait_recv()
        for half in range(2):
            b = 2 * s + half
            mine = upd[b, :, my_lanes(core)].astype(f32)
            theirs = sib[b].astype(f32)
            am_first = core == half
            later = jnp.where(am_first, pace[1, b : b + 1], pace[0, b : b + 1])
            comp[b] = (
                later * jnp.where(am_first, mine, theirs) + jnp.where(am_first, theirs, mine)
            ).astype(bf16)
        each_fellow(lambda i: send_update(s, i).start())
        keep_update(s).start()

    first = 128

    def intra(b, carry):
        scores = jnp.where(causal, by_rows(cs[b], bs[b]), 0.0)
        low_half = lax.broadcasted_iota(jnp.int32, (1, 128), 1) < HEAD_DIM
        for p in range(heads // 2):
            tops, ends = [], []
            for h in (2 * p, 2 * p + 1):
                col = cum_col[b, :, h : h + 1]
                row = cum_row[b, h : h + 1]
                size = dt_row[b, h : h + 1]
                gap = jnp.minimum(col[:first] - row[:, :first], 0.0)
                tops.append(
                    (scores[:first, :first] * jnp.exp(gap) * size[:, :first]).astype(bf16)
                )
                gap = jnp.minimum(col[first:] - row, 0.0)
                ends.append((scores[first:] * jnp.exp(gap) * size).astype(bf16))
            pair = slice(128 * p, 128 * p + 128)
            top = jnp.dot(
                jnp.concatenate(tops, axis=0), xs[b, :first, pair], preferred_element_type=f32
            )
            end = jnp.dot(
                jnp.concatenate(ends, axis=0), xs[b, :, pair], preferred_element_type=f32
            )
            inner[b, :first, pair] = jnp.where(low_half, top[:first], top[first:])
            rest = HALF - first
            inner[b, first:, pair] = jnp.where(low_half, end[:rest], end[rest:])
        return carry

    def chain(s):
        each_fellow(lambda i: send_update(s, i).wait_recv())
        keep_update(s).wait()
        state = jnp.zeros((state_rows, lanes), f32)
        for i in range(16):
            c, half = (i, 0) if i < 8 else (15 - i, 1)
            b = 2 * s + half
            back[c, b] = state.astype(bf16)
            state = steps[8 * c + b : 8 * c + b + 1] * state + got[c, b].astype(f32)
        each_fellow(lambda i: send_entry(s, i).start())
        keep_entry(s).start()

    def enter(s):
        each_fellow(lambda i: send_entry(s, i).wait_recv())
        keep_entry(s).wait()
        for half in range(2):
            b = 2 * s + half
            mine = upd[b, :, my_lanes(core)].astype(f32)
            theirs = sib[b].astype(f32)
            am_first = core == half
            entry = came[b].astype(f32)
            rate_first = jnp.where(am_first, pace[0, b : b + 1], pace[1, b : b + 1])
            second = rate_first * entry + jnp.where(am_first, mine, theirs)
            ent[b, :, my_lanes(core)] = jnp.where(am_first, entry, second).astype(bf16)
            give[b] = jnp.where(am_first, second, entry).astype(bf16)
        give_entry(s).start()

    def tile_rows(t):
        return pl.ds(pl.multiple_of(t * HALF, HALF), HALF)

    def to_partner(t):
        return remote(
            act.at[tile_rows(t), pl.ds(0, depth)], act.at[tile_rows(t), pl.ds(depth, depth)],
            y_s.at[t], y_r.at[t], across_y,
        )

    def finish(b, carry):
        squares = [jnp.zeros((96, 128), f32)] * 2
        for q in range(cols // chunk):
            part_cols = slice(q * chunk, (q + 1) * chunk)
            for i in range(2):
                r = slice(96 * i, 96 * i + 96)
                carried = jnp.dot(cs[b, r], ent[b, :, part_cols], preferred_element_type=f32)
                factor = jnp.dot(cum3[b, r], spread3[:, part_cols], preferred_element_type=f32)
                total = inner[b, r, part_cols] + factor * carried
                total = total + skips[:, part_cols] * xs[b, r, part_cols].astype(f32)
                gate = zbuf[b, r, part_cols].astype(f32)
                total = total * (gate / (1.0 + jnp.exp(-gate)))
                inner[b, r, part_cols] = total
                square = total * total
                squares[i] = squares[i] + square[:, :128] + square[:, 128:]
        for i in range(2):
            spread = jnp.sum(squares[i], axis=1, keepdims=True) * (1.0 / cols)
            scale = lax.rsqrt(spread + 1e-05)
            r = slice(96 * i, 96 * i + 96)
            to = pl.ds(pl.multiple_of(b * HALF + 96 * i, 96), 96)
            for q in range(cols // chunk):
                part_cols = slice(q * chunk, (q + 1) * chunk)
                act[to, part_cols] = (
                    inner[b, r, part_cols] * scale * gain_ref[:, part_cols]
                ).astype(bf16)
        to_partner(b).start()
        return carry

    def pass_on(t, way):
        return remote(
            mid.at[way, tile_rows(t)], relay.at[way, tile_rows(t)], mid_s.at[t, way],
            mid_r.at[t, way], ways[way],
        )

    def send_direct(t, way):
        return remote(
            direct.at[way, tile_rows(t)], final.at[way, 0, tile_rows(t)], fin_s.at[t, way, 0],
            fin_r.at[t, way, 0], ways[way],
        )

    def send_joined(t, way):
        return remote(
            joined.at[way, tile_rows(t)], final.at[way, 1, tile_rows(t)], fin_s.at[t, way, 1],
            fin_r.at[t, way, 1], ways[way],
        )

    def side_of(side):
        return slice(side * side_cols, (side + 1) * side_cols)

    def product(t, d, side):
        return jnp.dot(
            act[tile_rows(t)], wts[d, :, side_of(side)], preferred_element_type=f32
        )

    def project_far(t):
        to_partner(t).wait_recv()
        for way in range(2):
            mid[way, tile_rows(t)] = product(t, 0, way).astype(bf16)
            pass_on(t, way).start()

    def project_near(t, way):
        direct[way, tile_rows(t)] = product(t, 1 + way, 1 - way).astype(bf16)
        send_direct(t, way).start()
        keep[way, tile_rows(t)] = product(t, 1 + way, way)

    def project_join(t):
        for way in range(2):
            pass_on(t, way).wait_recv()
            r = tile_rows(t)
            joined[way, r] = (keep[way, r] + relay[way, r].astype(f32)).astype(bf16)
            send_joined(t, way).start()

    def project_own(t):
        for side in range(2):
            own[tile_rows(t), side_of(side)] = product(t, 3, side)

    def project_end(t):
        r = tile_rows(t)
        for way in range(2):
            send_direct(t, way).wait_recv()
            send_joined(t, way).wait_recv()
        for side in range(2):
            total = own[r, side_of(side)] + final[0, 1 - side, r].astype(f32)
            total = total + final[1, side, r].astype(f32)
            out_ref[r, side_of(side)] = total.astype(bf16)

    def loop(start, stop, work):
        lax.fori_loop(start, stop, work, 0)

    for half in range(2):
        for copy in halo(half):
            copy.wait_recv()
    loop(0, 2, front)
    swap_update(0).start()
    chip_decays()
    weights_in(0)
    weights_near(0, 0)
    loop(2, 3, front)
    join(0)
    weights_in(1)
    weights_near(0, 1)
    loop(3, 4, front)
    swap_update(1).start()
    loop(0, 1, intra)
    join(1)
    weights_in(2)
    weights_in(3)
    loop(1, 2, intra)
    each_fellow(lambda i: send_decay(i).wait_recv())
    steps[...] = to_lanes(decs[...].reshape(64, 128))
    chain(0)
    weights_far(0)
    loop(2, 3, intra)
    chain(1)
    weights_near(1, 0)
    weights_near(1, 1)
    z_copy.wait()
    enter(0)
    weights_last(0)
    loop(3, 4, intra)
    give_entry(0).wait_recv()
    loop(0, 2, finish)
    weights_near(2, 0)
    weights_near(2, 1)
    enter(1)
    weights_far(1)
    give_entry(1).wait_recv()
    loop(2, 4, finish)
    weights_far(2)
    weights_last(1)
    weights_near(3, 0)
    weights_near(3, 1)
    weights_ready(0)
    project_far(0)
    weights_last(2)
    weights_ready(1)
    project_near(0, 0)
    weights_ready(2)
    project_near(0, 1)
    weights_far(3)
    project_join(0)
    project_far(1)
    project_near(1, 0)
    project_near(1, 1)
    weights_last(3)
    weights_ready(3)

    def middle(t, carry):
        project_far(t)
        project_join(t - 1)
        project_near(t, 0)
        project_near(t, 1)
        project_own(t - 2)
        return carry

    loop(2, tiles, middle)
    project_join(tiles - 1)

    def rest(t, carry):
        project_own(t)
        return carry

    loop(tiles - 2, tiles, rest)

    for half in range(2):
        for copy in halo(half):
            copy.wait_send()
    swap_decay().wait_send()
    for s in range(2):
        swap_update(s).wait_send()
        give_entry(s).wait_send()

    def drain(i):
        send_decay(i).wait_send()
        for s in range(2):
            send_update(s, i).wait_send()
            send_entry(s, i).wait_send()

    each_fellow(drain)
    for d in range(4):
        import_part(d).wait_send()
        swap_part(d).wait_send()
        for way in range(2):
            far(d, way).wait_send()
            for swapped in range(2):
                near(d, way, swapped).wait_send()
        for number in range(5):
            across(d, number).wait_send()

    def last(t, carry):
        to_partner(t).wait_send()
        for way in range(2):
            pass_on(t, way).wait_send()
            send_direct(t, way).wait_send()
        project_end(t)
        for way in range(2):
            send_joined(t, way).wait_send()
        return carry

    loop(0, tiles, last)


def mix(x_part, bc_part, dt_part, a_log, skip_scale, norm_gain, conv_x, conv_bc, z_part, weight):
    blocks = 4
    heads = dt_part.shape[1]
    cols = x_part.shape[3]
    depth = weight.shape[0]
    tokens = blocks * HALF
    half = cols // 2
    dma = pltpu.SemaphoreType.DMA
    low, wide = jnp.bfloat16, jnp.float32
    vmem = pl.BlockSpec(memory_space=pltpu.VMEM)
    hbm = pl.BlockSpec(memory_space=pl.ANY)
    return pl.pallas_call(
        mixer_kernel,
        out_shape=jax.ShapeDtypeStruct((tokens, cols), low),
        in_specs=[vmem] * 8 + [hbm] * 2,
        out_specs=vmem,
        scratch_shapes=[
            pltpu.VMEM((2, 2, 16, cols), low),
            pltpu.VMEM((2, 2, 16, 2 * STATE), low),
            pltpu.VMEM((8 + HALF, 256), wide),
            pltpu.VMEM((blocks, HALF, cols), low),
            pltpu.VMEM((blocks, HALF, STATE), low),
            pltpu.VMEM((blocks, HALF, STATE), low),
            pltpu.VMEM((blocks, heads, HALF), wide),
            pltpu.VMEM((blocks, heads, HALF), wide),
            pltpu.VMEM((blocks, HALF, heads), wide),
            pltpu.VMEM((blocks, HALF, 3 * heads), low),
            pltpu.VMEM((blocks, HALF, 3 * heads), low),
            pltpu.VMEM((3 * heads, cols), low),
            pltpu.VMEM((1, cols), wide),
            pltpu.VMEM((HALF, 256), low),
            pltpu.VMEM((blocks, STATE, cols), low),
            pltpu.VMEM((blocks, STATE, half), low),
            pltpu.VMEM((blocks, STATE, half), low),
            pltpu.VMEM((8, blocks, STATE // 8, half), low),
            pltpu.VMEM((8, blocks, STATE // 8, half), low),
            pltpu.VMEM((blocks, STATE, half), low),
            pltpu.VMEM((blocks, STATE, half), low),
            pltpu.VMEM((blocks, STATE, cols), low),
            pltpu.VMEM((8, 128), wide),
            pltpu.VMEM((8, 128), wide),
            pltpu.VMEM((8, 128), wide),
            pltpu.VMEM((8, 8, 128), wide),
            pltpu.VMEM((64, half), wide),
            pltpu.VMEM((2, 8, half), wide),
            pltpu.VMEM((blocks, HALF, cols), wide),
            pltpu.VMEM((blocks, HALF, cols), low),
            pltpu.VMEM((tokens, 2 * depth), low),
            pltpu.VMEM((4, 2 * depth, cols), low),
            pltpu.VMEM((2, tokens, half), low),
            pltpu.VMEM((2, tokens, half), wide),
            pltpu.VMEM((2, tokens, half), low),
            pltpu.VMEM((2, tokens, half), low),
            pltpu.VMEM((tokens, cols), wide),
            pltpu.VMEM((2, tokens, half), low),
            pltpu.VMEM((2, 2, tokens, half), low),
            dma, dma((4,)), dma((2, 2)), dma((2, 2)), dma((8,)), dma((8,)), dma((2, 2)),
            dma((2,)), dma((2,)), dma((2, 8)), dma((2, 8)), dma((2, 8)), dma((2, 8)),
            dma((2,)), dma((2,)), dma((4,)), dma((4,)), dma((4,)), dma((4,)),
            dma((4, 2, 2)), dma((4, 2, 2)), dma((4, 2)), dma((4, 2)), dma((4, 5)), dma((4, 5)),
            dma((blocks,)), dma((blocks,)), dma((blocks, 2)), dma((blocks, 2)),
            dma((blocks, 2, 2)), dma((blocks, 2, 2)),
        ],
        compiler_params=pltpu.CompilerParams(
            collective_id=1, has_side_effects=True, vmem_limit_bytes=60 << 20
        ),
        name="mixer",
    )(x_part, bc_part, dt_part, a_log, skip_scale, norm_gain, conv_x, conv_bc, z_part, weight)


def mixer(
    x_part, z_part, bc_part, conv_x, conv_bc, dt_part, a_log, skip_scale, norm_gain, out_weight
):
    seq_count, tok_count, cols = x_part.shape
    heads = a_log.shape[0]
    projected = mix(
        x_part.reshape(seq_count, 2, HALF, cols),
        bc_part.reshape(seq_count, 2, HALF, 2 * STATE),
        dt_part,
        a_log.reshape(1, heads),
        skip_scale.reshape(1, heads),
        norm_gain.reshape(1, cols),
        conv_x,
        conv_bc,
        z_part.reshape(2 * seq_count, HALF, cols),
        out_weight,
    )
    return projected.reshape(seq_count, tok_count, cols)


def body(x_in, z_in, bc_in, conv_x, conv_bc, dt_raw, a_log, skip_scale, norm_gain, out_weight):
    return mixer(
        x_in, z_in, bc_in, conv_x, conv_bc, dt_raw, a_log, skip_scale, norm_gain, out_weight
    )


def solution(mesh):
    in_specs = (
        P(None, "ctx", "head"),
        P(None, "ctx", "head"),
        P(None, "ctx", None, "head"),
        P(None, "head"),
        P(None, None, "head"),
        P(None, "head", "ctx"),
        P("head"),
        P("head"),
        P("head"),
        P("head", None),
    )
    out_specs = P(None, "ctx", "head")
    return jax.shard_map(body, mesh=mesh, in_specs=in_specs, out_specs=out_specs, check_vma=False)
```

```python
import jax
import jax.numpy as jnp
from jax import lax
from jax.experimental import pallas as pl
from jax.experimental.pallas import tpu as pltpu
from jax.sharding import PartitionSpec as P

HEAD_DIM = 64
STATE = 128
KW = 4
HALF = 192
MESH = pl.DeviceIdType.MESH
REACH = (2, 1, 3, 0)


def place():
    c, h = lax.axis_index("ctx"), lax.axis_index("head")
    return c // 4, (c // 2) % 2, c % 2, h // 2, h % 2


def device(z, y_lo, core, x, y_hi):
    return (z * 4 + y_lo * 2 + core, x * 2 + y_hi)


def remote(src, dst, send_sem, recv_sem, target):
    return pltpu.make_async_remote_copy(
        src_ref=src,
        dst_ref=dst,
        send_sem=send_sem,
        recv_sem=recv_sem,
        device_id=target,
        device_id_type=MESH,
    )


def rounded_parts(values):
    high = values.astype(jnp.bfloat16)
    rest = values - high.astype(jnp.float32)
    middle = rest.astype(jnp.bfloat16)
    low = (rest - middle.astype(jnp.float32)).astype(jnp.bfloat16)
    return jnp.concatenate([high, middle, low], axis=0)


def unit(size):
    rows = lax.broadcasted_iota(jnp.int32, (size, size), 0)
    cols = lax.broadcasted_iota(jnp.int32, (size, size), 1)
    return jnp.where(rows == cols, 1.0, 0.0).astype(jnp.bfloat16)


def by_rows(left, right):
    return lax.dot_general(
        left, right, (((1,), (1,)), ((), ())), preferred_element_type=jnp.float32
    )


def mixer_kernel(
    x_ref, bc_ref, dt_ref, a_ref, skip_ref, gain_ref, taps_ref, taps_bc_ref, z_ref, w_ref,
    out_ref,
    halo_x, halo_bc, wide, xs, bs, cs, cum_row, dt_row, cum_col, tail3, cum3, spread3, skips,
    scaled, upd, sib, comp, got, back, came, give, ent, dec, dec_sib, dec_chip, decs, steps, pace,
    inner, zbuf, act, wts, mid, keep, direct, joined, own, relay, final,
    z_sem, load_s, halo_s, halo_r, dec_s, dec_r, own_s, sib_s, sib_r, upd_s, upd_r, ent_s, ent_r,
    give_s, give_r, in_s, in_r, side_s, side_r, near_s, near_r, far_s, far_r, core_s, core_r,
    y_s, y_r, mid_s, mid_r, fin_s, fin_r,
):
    f32, bf16 = jnp.float32, jnp.bfloat16
    z, y_lo, core, x, y_hi = place()
    me = lax.axis_index("ctx")
    chip = me // 2
    head = lax.axis_index("head")
    cols = x_ref.shape[3]
    state_rows, lanes = got.shape[2:]
    heads = dt_ref.shape[1]
    depth = wts.shape[1] // 2
    part = depth // 16
    side_cols = cols // 2
    tiles = 4

    partner = device(z, 1 - y_lo, core, x, 1 - y_hi)
    across_y = device(z, y_lo, core, x, 1 - y_hi)
    up = device((z + 1) % 4, y_lo, core, x, y_hi)
    down = device((z + 3) % 4, y_lo, core, x, y_hi)
    beside = device(z, 1 - y_lo, core, x, y_hi)
    other = device(z, y_lo, 1 - core, x, y_hi)
    ways = (
        device(z, y_lo, core, (x + 1) % 4, y_hi),
        device(z, y_lo, core, (x + 3) % 4, y_hi),
    )

    def at(index):
        return (index, head)

    before, after = at((me + 15) % 16), at((me + 1) % 16)

    def fellow(step):
        return (chip + step) % 8

    def of_chip(number):
        return at(2 * number + core)

    def each_fellow(work):
        def step(i, carry):
            work(i)
            return carry

        lax.fori_loop(1, 8, step, 0)

    def load(d):
        block = 2 * ((x + REACH[d]) % 4) + y_hi
        src = w_ref.at[:, pl.ds(pl.multiple_of(block * cols, cols), cols)]
        return pltpu.make_async_copy(src, wts.at[d, pl.ds(0, depth)], load_s.at[d])

    def piece(step, low, base, count=1):
        number = (((z + step) % 4) * 2 + core) * 2 + low
        return pl.ds(pl.multiple_of(base + number * part, part), count * part)

    def import_part(d):
        block = 2 * ((x + REACH[d]) % 4) + 1 - y_hi
        rows = piece(0, 1 - y_lo, 0)
        src = w_ref.at[rows, pl.ds(pl.multiple_of(block * cols, cols), cols)]
        there = wts.at[d, piece(0, 1 - y_lo, depth)]
        return remote(src, there, in_s.at[d], in_r.at[d], partner)

    def swap_part(d):
        here = wts.at[d, piece(0, y_lo, depth)]
        return remote(here, here, side_s.at[d], side_r.at[d], beside)

    def near(d, way, swapped):
        here = wts.at[d, piece(0, 1 - y_lo if swapped else y_lo, depth)]
        return remote(
            here, here, near_s.at[d, way, swapped], near_r.at[d, way, swapped],
            down if way else up,
        )

    def far(d, way):
        here = wts.at[d, piece(1 if way else 3, way, depth)]
        return remote(here, here, far_s.at[d, way], far_r.at[d, way], down if way else up)

    def across(d, number):
        if number < 2:
            rows = piece(0, 1 - y_lo if number else y_lo, depth)
        else:
            rows = piece((1, 3, 2)[number - 2], 0, depth, 2)
        here = wts.at[d, rows]
        return remote(here, here, core_s.at[d, number], core_r.at[d, number], other)

    def weights_in(d):
        import_part(d).wait_recv()
        swap_part(d).start()
        across(d, 0).start()

    def weights_near(d, swapped):
        if swapped:
            swap_part(d).wait_recv()
            across(d, 1).start()
        for way in range(2):
            near(d, way, swapped).start()

    def weights_far(d):
        for way in range(2):
            for swapped in range(2):
                near(d, way, swapped).wait_recv()
            far(d, way).start()
            across(d, 2 if way else 3).start()

    def weights_last(d):
        far(d, 0).wait_recv()
        far(d, 1).wait_recv()
        across(d, 4).start()

    def weights_ready(d):
        load(d).wait()
        for number in range(5):
            across(d, number).wait_recv()

    def halo(half):
        target = before if half else after
        rows = pl.ds(HALF - 16, 16)
        return (
            remote(
                x_ref.at[:, half, rows], halo_x.at[half], halo_s.at[half, 0], halo_r.at[half, 0],
                target,
            ),
            remote(
                bc_ref.at[:, half, rows], halo_bc.at[half], halo_s.at[half, 1],
                halo_r.at[half, 1], target,
            ),
        )

    def share(number):
        return pl.ds(pl.multiple_of(number * state_rows, state_rows), state_rows)

    def my_lanes(which):
        return pl.ds(pl.multiple_of(which * lanes, lanes), lanes)

    def of_seq(s):
        return pl.ds(2 * s, 2)

    def swap_decay():
        return remote(dec, dec_sib, dec_s.at[0], dec_r.at[0], other)

    def send_decay(step):
        return remote(
            dec_chip, decs.at[chip], dec_s.at[step], dec_r.at[step], of_chip(fellow(step))
        )

    def swap_update(s):
        return remote(
            upd.at[of_seq(s), :, my_lanes(1 - core)], sib.at[of_seq(s)], sib_s.at[s], sib_r.at[s],
            other,
        )

    def send_update(s, step):
        owner = fellow(step)
        return remote(
            comp.at[of_seq(s), share(owner)], got.at[chip, of_seq(s)], upd_s.at[s, step],
            upd_r.at[s, step], of_chip(owner),
        )

    def send_entry(s, step):
        target = fellow(step)
        return remote(
            back.at[target, of_seq(s)], came.at[of_seq(s), share(chip)], ent_s.at[s, step],
            ent_r.at[s, step], of_chip(target),
        )

    def give_entry(s):
        return remote(
            give.at[of_seq(s)], ent.at[of_seq(s), :, my_lanes(core)], give_s.at[s], give_r.at[s],
            other,
        )

    def keep_update(s):
        return pltpu.make_async_copy(
            comp.at[of_seq(s), share(chip)], got.at[chip, of_seq(s)], own_s.at[s, 0]
        )

    def keep_entry(s):
        return pltpu.make_async_copy(
            back.at[chip, of_seq(s)], came.at[of_seq(s), share(chip)], own_s.at[s, 1]
        )

    z_copy = pltpu.make_async_copy(z_ref, zbuf, z_sem)
    z_copy.start()
    barrier = pltpu.get_barrier_semaphore()

    def hello(target):
        pl.semaphore_signal(barrier, inc=1, device_id=target, device_id_type=MESH)

    each_fellow(lambda i: hello(of_chip(fellow(i))))
    hello(at((me + 15 + 2 * core) % 16))
    for target in (other, partner, across_y) + ways:
        hello(target)

    row_id = lax.broadcasted_iota(jnp.int32, (HALF, HALF), 0)
    col_id = lax.broadcasted_iota(jnp.int32, (HALF, HALF), 1)
    causal = row_id >= col_id
    eye = unit(HALF)

    def three(values, count):
        return values[:count] + values[count : 2 * count] + values[2 * count :]

    def three_cols(values, count):
        return values[:, :count] + values[:, count : 2 * count] + values[:, 2 * count :]

    rate = -jnp.exp(three_cols(by_rows(unit(heads), rounded_parts(a_ref[...])), 1))
    dec[...] = jnp.zeros_like(dec)
    source = lax.broadcasted_iota(jnp.int32, (2 * HALF, HALF), 0)
    goal = lax.broadcasted_iota(jnp.int32, (2 * HALF, HALF), 1)
    def decays(s):
        raw = dt_ref[s]
        both = jnp.maximum(raw, 0.0) + jnp.log1p(jnp.exp(-jnp.abs(raw)))
        sizes = rounded_parts(both)
        falls = rounded_parts(both * rate)
        for half in range(2):
            b = 2 * s + half
            low = HALF * half
            pick = jnp.where(source == goal + low, 1.0, 0.0).astype(bf16)
            ahead = jnp.where((source >= low) & (source <= goal + low), 1.0, 0.0).astype(bf16)
            step_size = three(jnp.dot(sizes, pick, preferred_element_type=f32), heads)
            cum = three(jnp.dot(falls, ahead, preferred_element_type=f32), heads)
            dt_row[b] = step_size
            cum_row[b] = cum
            col = three_cols(by_rows(eye, rounded_parts(cum)), heads)
            cum_col[b] = col
            dec[b : b + 1, :heads] = jnp.exp(col[HALF - 1 :])
            tail = jnp.exp(cum[:, HALF - 1 :] - cum) * step_size
            tail3[b] = by_rows(eye, rounded_parts(tail)).astype(bf16)
            cum3[b] = by_rows(eye, rounded_parts(jnp.exp(cum))).astype(bf16)
    decays(0)
    pl.semaphore_wait(barrier, 13)
    for half in range(2):
        for copy in halo(half):
            copy.start()
    for d in range(4):
        import_part(d).start()
    decays(1)
    swap_decay().start()
    for d in range(4):
        load(d).start()
    of_head = lax.broadcasted_iota(jnp.int32, spread3.shape, 1) // HEAD_DIM
    of_part = lax.broadcasted_iota(jnp.int32, spread3.shape, 0) % heads
    spread3[...] = jnp.where(of_head == of_part, 1.0, 0.0).astype(bf16)
    skips[...] = three(
        jnp.dot(rounded_parts(skip_ref[...]), spread3[:heads], preferred_element_type=f32), 1
    )

    head_id = lax.broadcasted_iota(jnp.int32, (128, lanes), 0)
    lane_head = lax.broadcasted_iota(jnp.int32, (128, lanes), 1) // HEAD_DIM
    picks = jnp.where(head_id == lane_head + core * (lanes // HEAD_DIM), 1.0, 0.0).astype(bf16)

    def to_lanes(values):
        count = values.shape[0]
        return three(jnp.dot(rounded_parts(values), picks, preferred_element_type=f32), count)

    def chip_decays():
        swap_decay().wait_recv()
        dec_chip[...] = dec[...] * dec_sib[...]
        each_fellow(lambda i: send_decay(i).start())
        decs[chip] = dec_chip[...]
        pace[0] = to_lanes(dec[...])
        pace[1] = to_lanes(dec_sib[...])

    turn = unit(STATE)
    chunk = 256
    band = 64

    def convolve(tap, put):
        for r in range(0, HALF, band):
            total = tap[0:1] * wide[r + 5 : r + 5 + band]
            for k in range(1, KW):
                total = total + tap[k : k + 1] * wide[r + 5 + k : r + 5 + k + band]
            put(r, (total / (1.0 + jnp.exp(-total))).astype(bf16))

    def front(b, carry):
        s, half = b // 2, b % 2

        taps_bc = jnp.concatenate([taps_bc_ref[:, 0], taps_bc_ref[:, 1]], axis=1)

        def put_bc(r, values):
            bs[b, r : r + band] = values[:, :STATE]
            cs[b, r : r + band] = values[:, STATE:]

        def split(values):
            return jnp.concatenate([values[:, 0], values[:, 1]], axis=1).astype(f32)

        earlier = split(halo_bc[0, s])
        earlier = jnp.where(me == 0, jnp.zeros_like(earlier), earlier)
        turned = jnp.where(
            me == 15, split(bc_ref[s, 0, HALF - 16 :]), split(halo_bc[1, s])
        )
        wide[0:8] = jnp.where(half == 0, earlier, turned)[8:]
        wide[8:] = split(bc_ref[s, half])
        convolve(taps_bc, put_bc)
        bs_turned = by_rows(turn, bs[b]).astype(bf16)

        def columns(i, carry):
            start = pl.multiple_of(i * chunk, chunk)

            def put(r, values):
                xs[b, r : r + band, pl.ds(start, chunk)] = values

            here = pl.ds(start, chunk)
            earlier = halo_x[0, s, :, here]
            earlier = jnp.where(me == 0, jnp.zeros_like(earlier), earlier)
            turned = jnp.where(me == 15, x_ref[s, 0, HALF - 16 :, here], halo_x[1, s, :, here])
            wide[0:8] = jnp.where(half == 0, earlier, turned).astype(f32)[8:]
            wide[8:] = x_ref[s, half, :, here].astype(f32)
            convolve(taps_ref[:, here], put)
            for r in range(0, HALF, band):
                factor = jnp.dot(
                    tail3[b, r : r + band], spread3[:, pl.ds(start, chunk)],
                    preferred_element_type=f32,
                )
                scaled[r : r + band] = (
                    factor * xs[b, r : r + band, pl.ds(start, chunk)].astype(f32)
                ).astype(bf16)
            upd[b, :, pl.ds(start, chunk)] = jnp.dot(
                bs_turned, scaled[...], preferred_element_type=f32
            ).astype(bf16)
            return carry

        lax.fori_loop(0, cols // chunk, columns, 0)
        return carry

    def join(s):
        swap_update(s).wait_recv()
        for half in range(2):
            b = 2 * s + half
            mine = upd[b, :, my_lanes(core)].astype(f32)
            theirs = sib[b].astype(f32)
            am_first = core == half
            later = jnp.where(am_first, pace[1, b : b + 1], pace[0, b : b + 1])
            comp[b] = (
                later * jnp.where(am_first, mine, theirs) + jnp.where(am_first, theirs, mine)
            ).astype(bf16)
        each_fellow(lambda i: send_update(s, i).start())
        keep_update(s).start()

    first = 128

    def intra(b, carry):
        scores = jnp.where(causal, by_rows(cs[b], bs[b]), 0.0)
        low_half = lax.broadcasted_iota(jnp.int32, (1, 128), 1) < HEAD_DIM
        for p in range(heads // 2):
            tops, ends = [], []
            for h in (2 * p, 2 * p + 1):
                col = cum_col[b, :, h : h + 1]
                row = cum_row[b, h : h + 1]
                size = dt_row[b, h : h + 1]
                gap = jnp.minimum(col[:first] - row[:, :first], 0.0)
                tops.append(
                    (scores[:first, :first] * jnp.exp(gap) * size[:, :first]).astype(bf16)
                )
                gap = jnp.minimum(col[first:] - row, 0.0)
                ends.append((scores[first:] * jnp.exp(gap) * size).astype(bf16))
            pair = slice(128 * p, 128 * p + 128)
            top = jnp.dot(
                jnp.concatenate(tops, axis=0), xs[b, :first, pair], preferred_element_type=f32
            )
            end = jnp.dot(
                jnp.concatenate(ends, axis=0), xs[b, :, pair], preferred_element_type=f32
            )
            inner[b, :first, pair] = jnp.where(low_half, top[:first], top[first:])
            rest = HALF - first
            inner[b, first:, pair] = jnp.where(low_half, end[:rest], end[rest:])
        return carry

    def chain(s):
        each_fellow(lambda i: send_update(s, i).wait_recv())
        keep_update(s).wait()
        state = jnp.zeros((state_rows, lanes), f32)
        for i in range(16):
            c, half = (i, 0) if i < 8 else (15 - i, 1)
            b = 2 * s + half
            back[c, b] = state.astype(bf16)
            state = steps[8 * c + b : 8 * c + b + 1] * state + got[c, b].astype(f32)
        each_fellow(lambda i: send_entry(s, i).start())
        keep_entry(s).start()

    def enter(s):
        each_fellow(lambda i: send_entry(s, i).wait_recv())
        keep_entry(s).wait()
        for half in range(2):
            b = 2 * s + half
            mine = upd[b, :, my_lanes(core)].astype(f32)
            theirs = sib[b].astype(f32)
            am_first = core == half
            entry = came[b].astype(f32)
            rate_first = jnp.where(am_first, pace[0, b : b + 1], pace[1, b : b + 1])
            second = rate_first * entry + jnp.where(am_first, mine, theirs)
            ent[b, :, my_lanes(core)] = jnp.where(am_first, entry, second).astype(bf16)
            give[b] = jnp.where(am_first, second, entry).astype(bf16)
        give_entry(s).start()

    def tile_rows(t):
        return pl.ds(pl.multiple_of(t * HALF, HALF), HALF)

    def to_partner(t):
        return remote(
            act.at[tile_rows(t), pl.ds(0, depth)], act.at[tile_rows(t), pl.ds(depth, depth)],
            y_s.at[t], y_r.at[t], across_y,
        )

    def finish(b, carry):
        squares = [jnp.zeros((96, 128), f32)] * 2
        for q in range(cols // chunk):
            part_cols = slice(q * chunk, (q + 1) * chunk)
            for i in range(2):
                r = slice(96 * i, 96 * i + 96)
                carried = jnp.dot(cs[b, r], ent[b, :, part_cols], preferred_element_type=f32)
                factor = jnp.dot(cum3[b, r], spread3[:, part_cols], preferred_element_type=f32)
                total = inner[b, r, part_cols] + factor * carried
                total = total + skips[:, part_cols] * xs[b, r, part_cols].astype(f32)
                gate = zbuf[b, r, part_cols].astype(f32)
                total = total * (gate / (1.0 + jnp.exp(-gate)))
                inner[b, r, part_cols] = total
                square = total * total
                squares[i] = squares[i] + square[:, :128] + square[:, 128:]
        for i in range(2):
            spread = jnp.sum(squares[i], axis=1, keepdims=True) * (1.0 / cols)
            scale = lax.rsqrt(spread + 1e-05)
            r = slice(96 * i, 96 * i + 96)
            to = pl.ds(pl.multiple_of(b * HALF + 96 * i, 96), 96)
            for q in range(cols // chunk):
                part_cols = slice(q * chunk, (q + 1) * chunk)
                act[to, part_cols] = (
                    inner[b, r, part_cols] * scale * gain_ref[:, part_cols]
                ).astype(bf16)
        to_partner(b).start()
        return carry

    def pass_on(t, way):
        return remote(
            mid.at[way, tile_rows(t)], relay.at[way, tile_rows(t)], mid_s.at[t, way],
            mid_r.at[t, way], ways[way],
        )

    def send_direct(t, way):
        return remote(
            direct.at[way, tile_rows(t)], final.at[way, 0, tile_rows(t)], fin_s.at[t, way, 0],
            fin_r.at[t, way, 0], ways[way],
        )

    def send_joined(t, way):
        return remote(
            joined.at[way, tile_rows(t)], final.at[way, 1, tile_rows(t)], fin_s.at[t, way, 1],
            fin_r.at[t, way, 1], ways[way],
        )

    def side_of(side):
        return slice(side * side_cols, (side + 1) * side_cols)

    def product(t, d, side):
        return jnp.dot(
            act[tile_rows(t)], wts[d, :, side_of(side)], preferred_element_type=f32
        )

    def project_far(t):
        to_partner(t).wait_recv()
        for way in range(2):
            mid[way, tile_rows(t)] = product(t, 0, way).astype(bf16)
            pass_on(t, way).start()

    def project_near(t, way):
        direct[way, tile_rows(t)] = product(t, 1 + way, 1 - way).astype(bf16)
        send_direct(t, way).start()
        keep[way, tile_rows(t)] = product(t, 1 + way, way)

    def project_join(t):
        for way in range(2):
            pass_on(t, way).wait_recv()
            r = tile_rows(t)
            joined[way, r] = (keep[way, r] + relay[way, r].astype(f32)).astype(bf16)
            send_joined(t, way).start()

    def project_own(t):
        for side in range(2):
            own[tile_rows(t), side_of(side)] = product(t, 3, side)

    def project_end(t):
        r = tile_rows(t)
        for way in range(2):
            send_direct(t, way).wait_recv()
            send_joined(t, way).wait_recv()
        for side in range(2):
            total = own[r, side_of(side)] + final[0, 1 - side, r].astype(f32)
            total = total + final[1, side, r].astype(f32)
            out_ref[r, side_of(side)] = total.astype(bf16)

    def loop(start, stop, work):
        lax.fori_loop(start, stop, work, 0)

    for half in range(2):
        for copy in halo(half):
            copy.wait_recv()
    loop(0, 2, front)
    swap_update(0).start()
    chip_decays()
    weights_in(0)
    weights_near(0, 0)
    loop(2, 3, front)
    join(0)
    weights_in(1)
    weights_near(0, 1)
    loop(3, 4, front)
    swap_update(1).start()
    loop(0, 1, intra)
    join(1)
    weights_in(2)
    weights_in(3)
    loop(1, 2, intra)
    each_fellow(lambda i: send_decay(i).wait_recv())
    steps[...] = to_lanes(decs[...].reshape(64, 128))
    chain(0)
    weights_far(0)
    loop(2, 3, intra)
    chain(1)
    weights_near(1, 0)
    weights_near(1, 1)
    z_copy.wait()
    enter(0)
    weights_last(0)
    loop(3, 4, intra)
    give_entry(0).wait_recv()
    loop(0, 2, finish)
    weights_near(2, 0)
    weights_near(2, 1)
    enter(1)
    weights_far(1)
    give_entry(1).wait_recv()
    loop(2, 4, finish)
    weights_far(2)
    weights_last(1)
    weights_near(3, 0)
    weights_near(3, 1)
    weights_ready(0)
    project_far(0)
    weights_last(2)
    weights_ready(1)
    project_near(0, 0)
    weights_ready(2)
    project_near(0, 1)
    weights_far(3)
    project_join(0)
    project_far(1)
    project_near(1, 0)
    project_near(1, 1)
    weights_last(3)
    weights_ready(3)

    def middle(t, carry):
        project_far(t)
        project_join(t - 1)
        project_near(t, 0)
        project_near(t, 1)
        project_own(t - 2)
        return carry

    loop(2, tiles, middle)
    project_join(tiles - 1)

    def rest(t, carry):
        project_own(t)
        return carry

    loop(tiles - 2, tiles, rest)

    for half in range(2):
        for copy in halo(half):
            copy.wait_send()
    swap_decay().wait_send()
    for s in range(2):
        swap_update(s).wait_send()
        give_entry(s).wait_send()

    def drain(i):
        send_decay(i).wait_send()
        for s in range(2):
            send_update(s, i).wait_send()
            send_entry(s, i).wait_send()

    each_fellow(drain)
    for d in range(4):
        import_part(d).wait_send()
        swap_part(d).wait_send()
        for way in range(2):
            far(d, way).wait_send()
            for swapped in range(2):
                near(d, way, swapped).wait_send()
        for number in range(5):
            across(d, number).wait_send()

    def last(t, carry):
        to_partner(t).wait_send()
        for way in range(2):
            pass_on(t, way).wait_send()
            send_direct(t, way).wait_send()
        project_end(t)
        for way in range(2):
            send_joined(t, way).wait_send()
        return carry

    loop(0, tiles, last)


def mix(x_part, bc_part, dt_part, a_log, skip_scale, norm_gain, conv_x, conv_bc, z_part, weight):
    blocks = 4
    heads = dt_part.shape[1]
    cols = x_part.shape[3]
    depth = weight.shape[0]
    tokens = blocks * HALF
    half = cols // 2
    dma = pltpu.SemaphoreType.DMA
    low, wide = jnp.bfloat16, jnp.float32
    vmem = pl.BlockSpec(memory_space=pltpu.VMEM)
    hbm = pl.BlockSpec(memory_space=pl.ANY)
    return pl.pallas_call(
        mixer_kernel,
        out_shape=pltpu.VMEM((tokens, cols), low),
        in_specs=[vmem] * 8 + [hbm] * 2,
        out_specs=vmem,
        scratch_shapes=[
            pltpu.VMEM((2, 2, 16, cols), low),
            pltpu.VMEM((2, 2, 16, 2, STATE), low),
            pltpu.VMEM((8 + HALF, 256), wide),
            pltpu.VMEM((blocks, HALF, cols), low),
            pltpu.VMEM((blocks, HALF, STATE), low),
            pltpu.VMEM((blocks, HALF, STATE), low),
            pltpu.VMEM((blocks, heads, HALF), wide),
            pltpu.VMEM((blocks, heads, HALF), wide),
            pltpu.VMEM((blocks, HALF, heads), wide),
            pltpu.VMEM((blocks, HALF, 3 * heads), low),
            pltpu.VMEM((blocks, HALF, 3 * heads), low),
            pltpu.VMEM((3 * heads, cols), low),
            pltpu.VMEM((1, cols), wide),
            pltpu.VMEM((HALF, 256), low),
            pltpu.VMEM((blocks, STATE, cols), low),
            pltpu.VMEM((blocks, STATE, half), low),
            pltpu.VMEM((blocks, STATE, half), low),
            pltpu.VMEM((8, blocks, STATE // 8, half), low),
            pltpu.VMEM((8, blocks, STATE // 8, half), low),
            pltpu.VMEM((blocks, STATE, half), low),
            pltpu.VMEM((blocks, STATE, half), low),
            pltpu.VMEM((blocks, STATE, cols), low),
            pltpu.VMEM((8, 128), wide),
            pltpu.VMEM((8, 128), wide),
            pltpu.VMEM((8, 128), wide),
            pltpu.VMEM((8, 8, 128), wide),
            pltpu.VMEM((64, half), wide),
            pltpu.VMEM((2, 8, half), wide),
            pltpu.VMEM((blocks, HALF, cols), wide),
            pltpu.VMEM((blocks, HALF, cols), low),
            pltpu.VMEM((tokens, 2 * depth), low),
            pltpu.VMEM((4, 2 * depth, cols), low),
            pltpu.VMEM((2, tokens, half), low),
            pltpu.VMEM((2, tokens, half), wide),
            pltpu.VMEM((2, tokens, half), low),
            pltpu.VMEM((2, tokens, half), low),
            pltpu.VMEM((tokens, cols), wide),
            pltpu.VMEM((2, tokens, half), low),
            pltpu.VMEM((2, 2, tokens, half), low),
            dma, dma((4,)), dma((2, 2)), dma((2, 2)), dma((8,)), dma((8,)), dma((2, 2)),
            dma((2,)), dma((2,)), dma((2, 8)), dma((2, 8)), dma((2, 8)), dma((2, 8)),
            dma((2,)), dma((2,)), dma((4,)), dma((4,)), dma((4,)), dma((4,)),
            dma((4, 2, 2)), dma((4, 2, 2)), dma((4, 2)), dma((4, 2)), dma((4, 5)), dma((4, 5)),
            dma((blocks,)), dma((blocks,)), dma((blocks, 2)), dma((blocks, 2)),
            dma((blocks, 2, 2)), dma((blocks, 2, 2)),
        ],
        compiler_params=pltpu.CompilerParams(
            collective_id=1, has_side_effects=True, vmem_limit_bytes=58 << 20
        ),
        name="mixer",
    )(x_part, bc_part, dt_part, a_log, skip_scale, norm_gain, conv_x, conv_bc, z_part, weight)


def mixer(
    x_part, z_part, bc_part, conv_x, conv_bc, dt_part, a_log, skip_scale, norm_gain, out_weight
):
    seq_count, tok_count, cols = x_part.shape
    heads = a_log.shape[0]
    projected = mix(
        x_part.reshape(seq_count, 2, HALF, cols),
        bc_part.reshape(seq_count, 2, HALF, 2, STATE),
        dt_part,
        a_log.reshape(1, heads),
        skip_scale.reshape(1, heads),
        norm_gain.reshape(1, cols),
        conv_x,
        conv_bc,
        z_part.reshape(2 * seq_count, HALF, cols),
        out_weight,
    )
    return projected.reshape(seq_count, tok_count, cols)


def body(x_in, z_in, bc_in, conv_x, conv_bc, dt_raw, a_log, skip_scale, norm_gain, out_weight):
    return mixer(
        x_in, z_in, bc_in, conv_x, conv_bc, dt_raw, a_log, skip_scale, norm_gain, out_weight
    )


def solution(mesh):
    in_specs = (
        P(None, "ctx", "head"),
        P(None, "ctx", "head"),
        P(None, "ctx", None, "head"),
        P(None, "head"),
        P(None, None, "head"),
        P(None, "head", "ctx"),
        P("head"),
        P("head"),
        P("head"),
        P("head", None),
    )
    out_specs = P(None, "ctx", "head")
    return jax.shard_map(body, mesh=mesh, in_specs=in_specs, out_specs=out_specs, check_vma=False)
```

```python
import jax
import jax.numpy as jnp
from jax import lax
from jax.experimental import pallas as pl
from jax.experimental.pallas import tpu as pltpu
from jax.sharding import PartitionSpec as P

HEAD_DIM = 64
STATE = 128
KW = 4
HALF = 192
MESH = pl.DeviceIdType.MESH
REACH = (2, 1, 3, 0)


def place():
    c, h = lax.axis_index("ctx"), lax.axis_index("head")
    return c // 4, (c // 2) % 2, c % 2, h // 2, h % 2


def device(z, y_lo, core, x, y_hi):
    return (z * 4 + y_lo * 2 + core, x * 2 + y_hi)


def remote(src, dst, send_sem, recv_sem, target):
    return pltpu.make_async_remote_copy(
        src_ref=src,
        dst_ref=dst,
        send_sem=send_sem,
        recv_sem=recv_sem,
        device_id=target,
        device_id_type=MESH,
    )


def rounded_parts(values):
    high = values.astype(jnp.bfloat16)
    rest = values - high.astype(jnp.float32)
    middle = rest.astype(jnp.bfloat16)
    low = (rest - middle.astype(jnp.float32)).astype(jnp.bfloat16)
    return jnp.concatenate([high, middle, low], axis=0)


def unit(size):
    rows = lax.broadcasted_iota(jnp.int32, (size, size), 0)
    cols = lax.broadcasted_iota(jnp.int32, (size, size), 1)
    return jnp.where(rows == cols, 1.0, 0.0).astype(jnp.bfloat16)


def by_rows(left, right):
    return lax.dot_general(
        left, right, (((1,), (1,)), ((), ())), preferred_element_type=jnp.float32
    )


def mixer_kernel(
    x_ref, bc_ref, dt_ref, a_ref, skip_ref, gain_ref, taps_ref, taps_bc_ref, z_ref, w_ref,
    out_ref,
    xbuf, halo_x, halo_bc, wide, xs, bs, cs, cum_row, dt_row, cum_col, tail3, cum3, spread3, skips,
    scaled, upd, sib, comp, got, back, came, give, ent, dec, dec_sib, dec_chip, decs, steps, pace,
    inner, zbuf, act, wts, mid, keep, direct, joined, own, relay, final,
    x_sem, z_sem, load_s, halo_s, halo_r, dec_s, dec_r, own_s, sib_s, sib_r, upd_s, upd_r, ent_s, ent_r,
    give_s, give_r, in_s, in_r, side_s, side_r, near_s, near_r, far_s, far_r, core_s, core_r,
    y_s, y_r, mid_s, mid_r, fin_s, fin_r,
):
    f32, bf16 = jnp.float32, jnp.bfloat16
    z, y_lo, core, x, y_hi = place()
    me = lax.axis_index("ctx")
    chip = me // 2
    head = lax.axis_index("head")
    cols = x_ref.shape[3]
    state_rows, lanes = got.shape[2:]
    heads = dt_ref.shape[1]
    depth = wts.shape[1] // 2
    part = depth // 16
    side_cols = cols // 2
    tiles = 4

    partner = device(z, 1 - y_lo, core, x, 1 - y_hi)
    across_y = device(z, y_lo, core, x, 1 - y_hi)
    up = device((z + 1) % 4, y_lo, core, x, y_hi)
    down = device((z + 3) % 4, y_lo, core, x, y_hi)
    beside = device(z, 1 - y_lo, core, x, y_hi)
    other = device(z, y_lo, 1 - core, x, y_hi)
    ways = (
        device(z, y_lo, core, (x + 1) % 4, y_hi),
        device(z, y_lo, core, (x + 3) % 4, y_hi),
    )

    def at(index):
        return (index, head)

    before, after = at((me + 15) % 16), at((me + 1) % 16)

    def fellow(step):
        return (chip + step) % 8

    def of_chip(number):
        return at(2 * number + core)

    def each_fellow(work):
        def step(i, carry):
            work(i)
            return carry

        lax.fori_loop(1, 8, step, 0)

    def load(d):
        block = 2 * ((x + REACH[d]) % 4) + y_hi
        src = w_ref.at[:, pl.ds(pl.multiple_of(block * cols, cols), cols)]
        return pltpu.make_async_copy(src, wts.at[d, pl.ds(0, depth)], load_s.at[d])

    def piece(step, low, base, count=1):
        number = (((z + step) % 4) * 2 + core) * 2 + low
        return pl.ds(pl.multiple_of(base + number * part, part), count * part)

    def import_part(d):
        block = 2 * ((x + REACH[d]) % 4) + 1 - y_hi
        rows = piece(0, 1 - y_lo, 0)
        src = w_ref.at[rows, pl.ds(pl.multiple_of(block * cols, cols), cols)]
        there = wts.at[d, piece(0, 1 - y_lo, depth)]
        return remote(src, there, in_s.at[d], in_r.at[d], partner)

    def swap_part(d):
        here = wts.at[d, piece(0, y_lo, depth)]
        return remote(here, here, side_s.at[d], side_r.at[d], beside)

    def near(d, way, swapped):
        here = wts.at[d, piece(0, 1 - y_lo if swapped else y_lo, depth)]
        return remote(
            here, here, near_s.at[d, way, swapped], near_r.at[d, way, swapped],
            down if way else up,
        )

    def far(d, way):
        here = wts.at[d, piece(1 if way else 3, way, depth)]
        return remote(here, here, far_s.at[d, way], far_r.at[d, way], down if way else up)

    def across(d, number):
        if number < 2:
            rows = piece(0, 1 - y_lo if number else y_lo, depth)
        else:
            rows = piece((1, 3, 2)[number - 2], 0, depth, 2)
        here = wts.at[d, rows]
        return remote(here, here, core_s.at[d, number], core_r.at[d, number], other)

    def weights_in(d):
        import_part(d).wait_recv()
        swap_part(d).start()
        across(d, 0).start()

    def weights_near(d, swapped):
        if swapped:
            swap_part(d).wait_recv()
            across(d, 1).start()
        for way in range(2):
            near(d, way, swapped).start()

    def weights_far(d):
        for way in range(2):
            for swapped in range(2):
                near(d, way, swapped).wait_recv()
            far(d, way).start()
            across(d, 2 if way else 3).start()

    def weights_last(d):
        far(d, 0).wait_recv()
        far(d, 1).wait_recv()
        across(d, 4).start()

    def weights_ready(d):
        load(d).wait()
        for number in range(5):
            across(d, number).wait_recv()

    def halo(half):
        target = before if half else after
        rows = pl.ds(HALF - 16, 16)
        return (
            remote(
                xbuf.at[:, half, rows], halo_x.at[half], halo_s.at[half, 0], halo_r.at[half, 0],
                target,
            ),
            remote(
                bc_ref.at[:, half, rows], halo_bc.at[half], halo_s.at[half, 1],
                halo_r.at[half, 1], target,
            ),
        )

    def share(number):
        return pl.ds(pl.multiple_of(number * state_rows, state_rows), state_rows)

    def my_lanes(which):
        return pl.ds(pl.multiple_of(which * lanes, lanes), lanes)

    def of_seq(s):
        return pl.ds(2 * s, 2)

    def swap_decay():
        return remote(dec, dec_sib, dec_s.at[0], dec_r.at[0], other)

    def send_decay(step):
        return remote(
            dec_chip, decs.at[chip], dec_s.at[step], dec_r.at[step], of_chip(fellow(step))
        )

    def swap_update(s):
        return remote(
            upd.at[of_seq(s), :, my_lanes(1 - core)], sib.at[of_seq(s)], sib_s.at[s], sib_r.at[s],
            other,
        )

    def send_update(s, step):
        owner = fellow(step)
        return remote(
            comp.at[of_seq(s), share(owner)], got.at[chip, of_seq(s)], upd_s.at[s, step],
            upd_r.at[s, step], of_chip(owner),
        )

    def send_entry(s, step):
        target = fellow(step)
        return remote(
            back.at[target, of_seq(s)], came.at[of_seq(s), share(chip)], ent_s.at[s, step],
            ent_r.at[s, step], of_chip(target),
        )

    def give_entry(s):
        return remote(
            give.at[of_seq(s)], ent.at[of_seq(s), :, my_lanes(core)], give_s.at[s], give_r.at[s],
            other,
        )

    def keep_update(s):
        return pltpu.make_async_copy(
            comp.at[of_seq(s), share(chip)], got.at[chip, of_seq(s)], own_s.at[s, 0]
        )

    def keep_entry(s):
        return pltpu.make_async_copy(
            back.at[chip, of_seq(s)], came.at[of_seq(s), share(chip)], own_s.at[s, 1]
        )

    x_copy = pltpu.make_async_copy(x_ref, xbuf, x_sem)
    x_copy.start()
    z_copy = pltpu.make_async_copy(z_ref, zbuf, z_sem)
    z_copy.start()
    barrier = pltpu.get_barrier_semaphore()

    def hello(target):
        pl.semaphore_signal(barrier, inc=1, device_id=target, device_id_type=MESH)

    each_fellow(lambda i: hello(of_chip(fellow(i))))
    hello(at((me + 15 + 2 * core) % 16))
    for target in (other, partner, across_y) + ways:
        hello(target)

    row_id = lax.broadcasted_iota(jnp.int32, (HALF, HALF), 0)
    col_id = lax.broadcasted_iota(jnp.int32, (HALF, HALF), 1)
    causal = row_id >= col_id
    eye = unit(HALF)

    def three(values, count):
        return values[:count] + values[count : 2 * count] + values[2 * count :]

    def three_cols(values, count):
        return values[:, :count] + values[:, count : 2 * count] + values[:, 2 * count :]

    rate = -jnp.exp(three_cols(by_rows(unit(heads), rounded_parts(a_ref[...])), 1))
    dec[...] = jnp.zeros_like(dec)
    source = lax.broadcasted_iota(jnp.int32, (2 * HALF, HALF), 0)
    goal = lax.broadcasted_iota(jnp.int32, (2 * HALF, HALF), 1)
    def decays(s):
        raw = dt_ref[s]
        both = jnp.maximum(raw, 0.0) + jnp.log1p(jnp.exp(-jnp.abs(raw)))
        sizes = rounded_parts(both)
        falls = rounded_parts(both * rate)
        for half in range(2):
            b = 2 * s + half
            low = HALF * half
            pick = jnp.where(source == goal + low, 1.0, 0.0).astype(bf16)
            ahead = jnp.where((source >= low) & (source <= goal + low), 1.0, 0.0).astype(bf16)
            step_size = three(jnp.dot(sizes, pick, preferred_element_type=f32), heads)
            cum = three(jnp.dot(falls, ahead, preferred_element_type=f32), heads)
            dt_row[b] = step_size
            cum_row[b] = cum
            col = three_cols(by_rows(eye, rounded_parts(cum)), heads)
            cum_col[b] = col
            dec[b : b + 1, :heads] = jnp.exp(col[HALF - 1 :])
            tail = jnp.exp(cum[:, HALF - 1 :] - cum) * step_size
            tail3[b] = by_rows(eye, rounded_parts(tail)).astype(bf16)
            cum3[b] = by_rows(eye, rounded_parts(jnp.exp(cum))).astype(bf16)
    decays(0)
    x_copy.wait()
    pl.semaphore_wait(barrier, 13)
    for half in range(2):
        for copy in halo(half):
            copy.start()
    for d in range(4):
        import_part(d).start()
    decays(1)
    swap_decay().start()
    for d in range(4):
        load(d).start()
    of_head = lax.broadcasted_iota(jnp.int32, spread3.shape, 1) // HEAD_DIM
    of_part = lax.broadcasted_iota(jnp.int32, spread3.shape, 0) % heads
    spread3[...] = jnp.where(of_head == of_part, 1.0, 0.0).astype(bf16)
    skips[...] = three(
        jnp.dot(rounded_parts(skip_ref[...]), spread3[:heads], preferred_element_type=f32), 1
    )

    head_id = lax.broadcasted_iota(jnp.int32, (128, lanes), 0)
    lane_head = lax.broadcasted_iota(jnp.int32, (128, lanes), 1) // HEAD_DIM
    picks = jnp.where(head_id == lane_head + core * (lanes // HEAD_DIM), 1.0, 0.0).astype(bf16)

    def to_lanes(values):
        count = values.shape[0]
        return three(jnp.dot(rounded_parts(values), picks, preferred_element_type=f32), count)

    def chip_decays():
        swap_decay().wait_recv()
        dec_chip[...] = dec[...] * dec_sib[...]
        each_fellow(lambda i: send_decay(i).start())
        decs[chip] = dec_chip[...]
        pace[0] = to_lanes(dec[...])
        pace[1] = to_lanes(dec_sib[...])

    turn = unit(STATE)
    chunk = 256
    band = 64

    def convolve(tap, put):
        for r in range(0, HALF, band):
            total = tap[0:1] * wide[r + 5 : r + 5 + band]
            for k in range(1, KW):
                total = total + tap[k : k + 1] * wide[r + 5 + k : r + 5 + k + band]
            put(r, (total / (1.0 + jnp.exp(-total))).astype(bf16))

    def front(b, carry):
        s, half = b // 2, b % 2

        taps_bc = jnp.concatenate([taps_bc_ref[:, 0], taps_bc_ref[:, 1]], axis=1)

        def put_bc(r, values):
            bs[b, r : r + band] = values[:, :STATE]
            cs[b, r : r + band] = values[:, STATE:]

        def split(values):
            return jnp.concatenate([values[:, 0], values[:, 1]], axis=1).astype(f32)

        earlier = split(halo_bc[0, s])
        earlier = jnp.where(me == 0, jnp.zeros_like(earlier), earlier)
        turned = jnp.where(
            me == 15, split(bc_ref[s, 0, HALF - 16 :]), split(halo_bc[1, s])
        )
        wide[0:8] = jnp.where(half == 0, earlier, turned)[8:]
        wide[8:] = split(bc_ref[s, half])
        convolve(taps_bc, put_bc)
        bs_turned = by_rows(turn, bs[b]).astype(bf16)

        def columns(i, carry):
            start = pl.multiple_of(i * chunk, chunk)

            def put(r, values):
                xs[b, r : r + band, pl.ds(start, chunk)] = values

            here = pl.ds(start, chunk)
            earlier = halo_x[0, s, :, here]
            earlier = jnp.where(me == 0, jnp.zeros_like(earlier), earlier)
            turned = jnp.where(me == 15, xbuf[s, 0, HALF - 16 :, here], halo_x[1, s, :, here])
            wide[0:8] = jnp.where(half == 0, earlier, turned).astype(f32)[8:]
            wide[8:] = xbuf[s, half, :, here].astype(f32)
            convolve(taps_ref[:, here], put)
            for r in range(0, HALF, band):
                factor = jnp.dot(
                    tail3[b, r : r + band], spread3[:, pl.ds(start, chunk)],
                    preferred_element_type=f32,
                )
                scaled[r : r + band] = (
                    factor * xs[b, r : r + band, pl.ds(start, chunk)].astype(f32)
                ).astype(bf16)
            upd[b, :, pl.ds(start, chunk)] = jnp.dot(
                bs_turned, scaled[...], preferred_element_type=f32
            ).astype(bf16)
            return carry

        lax.fori_loop(0, cols // chunk, columns, 0)
        return carry

    def join(s):
        swap_update(s).wait_recv()
        for half in range(2):
            b = 2 * s + half
            mine = upd[b, :, my_lanes(core)].astype(f32)
            theirs = sib[b].astype(f32)
            am_first = core == half
            later = jnp.where(am_first, pace[1, b : b + 1], pace[0, b : b + 1])
            comp[b] = (
                later * jnp.where(am_first, mine, theirs) + jnp.where(am_first, theirs, mine)
            ).astype(bf16)
        each_fellow(lambda i: send_update(s, i).start())
        keep_update(s).start()

    first = 128

    def intra(b, carry):
        scores = jnp.where(causal, by_rows(cs[b], bs[b]), 0.0)
        low_half = lax.broadcasted_iota(jnp.int32, (1, 128), 1) < HEAD_DIM
        for p in range(heads // 2):
            tops, ends = [], []
            for h in (2 * p, 2 * p + 1):
                col = cum_col[b, :, h : h + 1]
                row = cum_row[b, h : h + 1]
                size = dt_row[b, h : h + 1]
                gap = jnp.minimum(col[:first] - row[:, :first], 0.0)
                tops.append(
                    (scores[:first, :first] * jnp.exp(gap) * size[:, :first]).astype(bf16)
                )
                gap = jnp.minimum(col[first:] - row, 0.0)
                ends.append((scores[first:] * jnp.exp(gap) * size).astype(bf16))
            pair = slice(128 * p, 128 * p + 128)
            top = jnp.dot(
                jnp.concatenate(tops, axis=0), xs[b, :first, pair], preferred_element_type=f32
            )
            end = jnp.dot(
                jnp.concatenate(ends, axis=0), xs[b, :, pair], preferred_element_type=f32
            )
            inner[b, :first, pair] = jnp.where(low_half, top[:first], top[first:])
            rest = HALF - first
            inner[b, first:, pair] = jnp.where(low_half, end[:rest], end[rest:])
        return carry

    def chain(s):
        each_fellow(lambda i: send_update(s, i).wait_recv())
        keep_update(s).wait()
        state = jnp.zeros((state_rows, lanes), f32)
        for i in range(16):
            c, half = (i, 0) if i < 8 else (15 - i, 1)
            b = 2 * s + half
            back[c, b] = state.astype(bf16)
            state = steps[8 * c + b : 8 * c + b + 1] * state + got[c, b].astype(f32)
        each_fellow(lambda i: send_entry(s, i).start())
        keep_entry(s).start()

    def enter(s):
        each_fellow(lambda i: send_entry(s, i).wait_recv())
        keep_entry(s).wait()
        for half in range(2):
            b = 2 * s + half
            mine = upd[b, :, my_lanes(core)].astype(f32)
            theirs = sib[b].astype(f32)
            am_first = core == half
            entry = came[b].astype(f32)
            rate_first = jnp.where(am_first, pace[0, b : b + 1], pace[1, b : b + 1])
            second = rate_first * entry + jnp.where(am_first, mine, theirs)
            ent[b, :, my_lanes(core)] = jnp.where(am_first, entry, second).astype(bf16)
            give[b] = jnp.where(am_first, second, entry).astype(bf16)
        give_entry(s).start()

    def tile_rows(t):
        return pl.ds(pl.multiple_of(t * HALF, HALF), HALF)

    def to_partner(t):
        return remote(
            act.at[tile_rows(t), pl.ds(0, depth)], act.at[tile_rows(t), pl.ds(depth, depth)],
            y_s.at[t], y_r.at[t], across_y,
        )

    def finish(b, carry):
        squares = [jnp.zeros((96, 128), f32)] * 2
        for q in range(cols // chunk):
            part_cols = slice(q * chunk, (q + 1) * chunk)
            for i in range(2):
                r = slice(96 * i, 96 * i + 96)
                carried = jnp.dot(cs[b, r], ent[b, :, part_cols], preferred_element_type=f32)
                factor = jnp.dot(cum3[b, r], spread3[:, part_cols], preferred_element_type=f32)
                total = inner[b, r, part_cols] + factor * carried
                total = total + skips[:, part_cols] * xs[b, r, part_cols].astype(f32)
                gate = zbuf[b, r, part_cols].astype(f32)
                total = total * (gate / (1.0 + jnp.exp(-gate)))
                inner[b, r, part_cols] = total
                square = total * total
                squares[i] = squares[i] + square[:, :128] + square[:, 128:]
        for i in range(2):
            spread = jnp.sum(squares[i], axis=1, keepdims=True) * (1.0 / cols)
            scale = lax.rsqrt(spread + 1e-05)
            r = slice(96 * i, 96 * i + 96)
            to = pl.ds(pl.multiple_of(b * HALF + 96 * i, 96), 96)
            for q in range(cols // chunk):
                part_cols = slice(q * chunk, (q + 1) * chunk)
                act[to, part_cols] = (
                    inner[b, r, part_cols] * scale * gain_ref[:, part_cols]
                ).astype(bf16)
        to_partner(b).start()
        return carry

    def pass_on(t, way):
        return remote(
            mid.at[way, tile_rows(t)], relay.at[way, tile_rows(t)], mid_s.at[t, way],
            mid_r.at[t, way], ways[way],
        )

    def send_direct(t, way):
        return remote(
            direct.at[way, tile_rows(t)], final.at[way, 0, tile_rows(t)], fin_s.at[t, way, 0],
            fin_r.at[t, way, 0], ways[way],
        )

    def send_joined(t, way):
        return remote(
            joined.at[way, tile_rows(t)], final.at[way, 1, tile_rows(t)], fin_s.at[t, way, 1],
            fin_r.at[t, way, 1], ways[way],
        )

    def side_of(side):
        return slice(side * side_cols, (side + 1) * side_cols)

    def product(t, d, side):
        return jnp.dot(
            act[tile_rows(t)], wts[d, :, side_of(side)], preferred_element_type=f32
        )

    def project_far(t):
        to_partner(t).wait_recv()
        for way in range(2):
            mid[way, tile_rows(t)] = product(t, 0, way).astype(bf16)
            pass_on(t, way).start()

    def project_near(t, way):
        direct[way, tile_rows(t)] = product(t, 1 + way, 1 - way).astype(bf16)
        send_direct(t, way).start()
        keep[way, tile_rows(t)] = product(t, 1 + way, way)

    def project_join(t):
        for way in range(2):
            pass_on(t, way).wait_recv()
            r = tile_rows(t)
            joined[way, r] = (keep[way, r] + relay[way, r].astype(f32)).astype(bf16)
            send_joined(t, way).start()

    def project_own(t):
        for side in range(2):
            own[tile_rows(t), side_of(side)] = product(t, 3, side)

    def project_end(t):
        r = tile_rows(t)
        for way in range(2):
            send_direct(t, way).wait_recv()
            send_joined(t, way).wait_recv()
        for side in range(2):
            total = own[r, side_of(side)] + final[0, 1 - side, r].astype(f32)
            total = total + final[1, side, r].astype(f32)
            out_ref[r, side_of(side)] = total.astype(bf16)

    def loop(start, stop, work):
        lax.fori_loop(start, stop, work, 0)

    for half in range(2):
        for copy in halo(half):
            copy.wait_recv()
    loop(0, 2, front)
    swap_update(0).start()
    chip_decays()
    weights_in(0)
    weights_near(0, 0)
    loop(2, 3, front)
    join(0)
    weights_in(1)
    weights_near(0, 1)
    loop(3, 4, front)
    swap_update(1).start()
    loop(0, 1, intra)
    join(1)
    weights_in(2)
    weights_in(3)
    loop(1, 2, intra)
    each_fellow(lambda i: send_decay(i).wait_recv())
    steps[...] = to_lanes(decs[...].reshape(64, 128))
    chain(0)
    weights_far(0)
    loop(2, 3, intra)
    chain(1)
    weights_near(1, 0)
    weights_near(1, 1)
    z_copy.wait()
    enter(0)
    weights_last(0)
    loop(3, 4, intra)
    give_entry(0).wait_recv()
    loop(0, 2, finish)
    weights_near(2, 0)
    weights_near(2, 1)
    enter(1)
    weights_far(1)
    give_entry(1).wait_recv()
    loop(2, 4, finish)
    weights_far(2)
    weights_last(1)
    weights_near(3, 0)
    weights_near(3, 1)
    weights_ready(0)
    project_far(0)
    weights_last(2)
    weights_ready(1)
    project_near(0, 0)
    weights_ready(2)
    project_near(0, 1)
    weights_far(3)
    project_join(0)
    project_far(1)
    project_near(1, 0)
    project_near(1, 1)
    weights_last(3)
    weights_ready(3)

    def middle(t, carry):
        project_far(t)
        project_join(t - 1)
        project_near(t, 0)
        project_near(t, 1)
        project_own(t - 2)
        return carry

    loop(2, tiles, middle)
    project_join(tiles - 1)

    def rest(t, carry):
        project_own(t)
        return carry

    loop(tiles - 2, tiles, rest)

    for half in range(2):
        for copy in halo(half):
            copy.wait_send()
    swap_decay().wait_send()
    for s in range(2):
        swap_update(s).wait_send()
        give_entry(s).wait_send()

    def drain(i):
        send_decay(i).wait_send()
        for s in range(2):
            send_update(s, i).wait_send()
            send_entry(s, i).wait_send()

    each_fellow(drain)
    for d in range(4):
        import_part(d).wait_send()
        swap_part(d).wait_send()
        for way in range(2):
            far(d, way).wait_send()
            for swapped in range(2):
                near(d, way, swapped).wait_send()
        for number in range(5):
            across(d, number).wait_send()

    def last(t, carry):
        to_partner(t).wait_send()
        for way in range(2):
            pass_on(t, way).wait_send()
            send_direct(t, way).wait_send()
        project_end(t)
        for way in range(2):
            send_joined(t, way).wait_send()
        return carry

    loop(0, tiles, last)


def mix(x_part, bc_part, dt_part, a_log, skip_scale, norm_gain, conv_x, conv_bc, z_part, weight):
    blocks = 4
    heads = dt_part.shape[1]
    cols = x_part.shape[3]
    depth = weight.shape[0]
    tokens = blocks * HALF
    half = cols // 2
    dma = pltpu.SemaphoreType.DMA
    low, wide = jnp.bfloat16, jnp.float32
    vmem = pl.BlockSpec(memory_space=pltpu.VMEM)
    hbm = pl.BlockSpec(memory_space=pl.ANY)
    return pl.pallas_call(
        mixer_kernel,
        out_shape=pltpu.VMEM((tokens, cols), low),
        in_specs=[hbm] + [vmem] * 7 + [hbm] * 2,
        out_specs=vmem,
        scratch_shapes=[
            pltpu.VMEM((2, 2, HALF, cols), low),
            pltpu.VMEM((2, 2, 16, cols), low),
            pltpu.VMEM((2, 2, 16, 2, STATE), low),
            pltpu.VMEM((8 + HALF, 256), wide),
            pltpu.VMEM((blocks, HALF, cols), low),
            pltpu.VMEM((blocks, HALF, STATE), low),
            pltpu.VMEM((blocks, HALF, STATE), low),
            pltpu.VMEM((blocks, heads, HALF), wide),
            pltpu.VMEM((blocks, heads, HALF), wide),
            pltpu.VMEM((blocks, HALF, heads), wide),
            pltpu.VMEM((blocks, HALF, 3 * heads), low),
            pltpu.VMEM((blocks, HALF, 3 * heads), low),
            pltpu.VMEM((3 * heads, cols), low),
            pltpu.VMEM((1, cols), wide),
            pltpu.VMEM((HALF, 256), low),
            pltpu.VMEM((blocks, STATE, cols), low),
            pltpu.VMEM((blocks, STATE, half), low),
            pltpu.VMEM((blocks, STATE, half), low),
            pltpu.VMEM((8, blocks, STATE // 8, half), low),
            pltpu.VMEM((8, blocks, STATE // 8, half), low),
            pltpu.VMEM((blocks, STATE, half), low),
            pltpu.VMEM((blocks, STATE, half), low),
            pltpu.VMEM((blocks, STATE, cols), low),
            pltpu.VMEM((8, 128), wide),
            pltpu.VMEM((8, 128), wide),
            pltpu.VMEM((8, 128), wide),
            pltpu.VMEM((8, 8, 128), wide),
            pltpu.VMEM((64, half), wide),
            pltpu.VMEM((2, 8, half), wide),
            pltpu.VMEM((blocks, HALF, cols), wide),
            pltpu.VMEM((blocks, HALF, cols), low),
            pltpu.VMEM((tokens, 2 * depth), low),
            pltpu.VMEM((4, 2 * depth, cols), low),
            pltpu.VMEM((2, tokens, half), low),
            pltpu.VMEM((2, tokens, half), wide),
            pltpu.VMEM((2, tokens, half), low),
            pltpu.VMEM((2, tokens, half), low),
            pltpu.VMEM((tokens, cols), wide),
            pltpu.VMEM((2, tokens, half), low),
            pltpu.VMEM((2, 2, tokens, half), low),
            dma, dma, dma((4,)), dma((2, 2)), dma((2, 2)), dma((8,)), dma((8,)), dma((2, 2)),
            dma((2,)), dma((2,)), dma((2, 8)), dma((2, 8)), dma((2, 8)), dma((2, 8)),
            dma((2,)), dma((2,)), dma((4,)), dma((4,)), dma((4,)), dma((4,)),
            dma((4, 2, 2)), dma((4, 2, 2)), dma((4, 2)), dma((4, 2)), dma((4, 5)), dma((4, 5)),
            dma((blocks,)), dma((blocks,)), dma((blocks, 2)), dma((blocks, 2)),
            dma((blocks, 2, 2)), dma((blocks, 2, 2)),
        ],
        compiler_params=pltpu.CompilerParams(
            collective_id=1, has_side_effects=True, vmem_limit_bytes=58 << 20
        ),
        name="mixer",
    )(x_part, bc_part, dt_part, a_log, skip_scale, norm_gain, conv_x, conv_bc, z_part, weight)


def mixer(
    x_part, z_part, bc_part, conv_x, conv_bc, dt_part, a_log, skip_scale, norm_gain, out_weight
):
    seq_count, tok_count, cols = x_part.shape
    heads = a_log.shape[0]
    projected = mix(
        x_part.reshape(seq_count, 2, HALF, cols),
        bc_part.reshape(seq_count, 2, HALF, 2, STATE),
        dt_part,
        a_log.reshape(1, heads),
        skip_scale.reshape(1, heads),
        norm_gain.reshape(1, cols),
        conv_x,
        conv_bc,
        z_part.reshape(2 * seq_count, HALF, cols),
        out_weight,
    )
    return projected.reshape(seq_count, tok_count, cols)


def body(x_in, z_in, bc_in, conv_x, conv_bc, dt_raw, a_log, skip_scale, norm_gain, out_weight):
    return mixer(
        x_in, z_in, bc_in, conv_x, conv_bc, dt_raw, a_log, skip_scale, norm_gain, out_weight
    )


def solution(mesh):
    in_specs = (
        P(None, "ctx", "head"),
        P(None, "ctx", "head"),
        P(None, "ctx", None, "head"),
        P(None, "head"),
        P(None, None, "head"),
        P(None, "head", "ctx"),
        P("head"),
        P("head"),
        P("head"),
        P("head", None),
    )
    out_specs = P(None, "ctx", "head")
    return jax.shard_map(body, mesh=mesh, in_specs=in_specs, out_specs=out_specs, check_vma=False)
```
